1024 devices in a mesh: gx: 256 (over z, y, core), gy: 4 (over x).
Axes of the slice: x: 4, y: 8, z: 16, core: 2. Of those that a mesh axis runs over, the one named last changes fastest.
Arguments:
- rhs: float32 [8, 512, 32, 128], P(None, 'gx', 'gy'), may hold values from -6 to 6
- classes: int32 [512, 32, 128], P('gx', 'gy'), may hold values from 0 to 3
- supports: int32 [512, 32, 128], P('gx', 'gy'), may hold values 0 or 1
Outputs:
- solution: float32 [8, 512, 32, 128], P(None, 'gx', 'gy')
- residual: float32 [8, 512, 32, 128], P(None, 'gx', 'gy')
- new_direction: float32 [8, 512, 32, 128], P(None, 'gx', 'gy')
The draws below stay inside these ranges and needn't reach their ends.
Inputs may be any that keep to these rules, and one draw needn't show every extreme that they name: `supports`: 1 marks a grounded node.
All inputs are finite; a program needn't handle non-finite values. No bound on the sum of `supports` on one device may be relied on, other than what follows from the above.
Results may differ from the reference program's by a relative error of at most 0.0003.
Values sent between devices are 32-bit elements; how exact they have to be, the bound alone decides.
No kernel may reach another device: no remote copies, remote signals or barrier semaphores. Data moves between devices by JAX's collectives and lax.ppermute only.
A program may use at most 32 MiB of HBM per device.

```python
import jax
import jax.numpy as jnp
from jax import lax

RHS = 8
COARSE_SWEEPS = 2
NX = 512
NY = 32
NZ = 128


def with_ends(values, own_key, least, top_value):
    dims = values.shape
    spot = [jax.random.randint(jax.random.fold_in(own_key, axis), (), 0, dims[axis]) for axis in range(len(dims))]
    values = values.at[tuple(spot)].set(least)
    longest = dims.index(max(dims))
    spot[longest] = (spot[longest] + 1) % dims[longest]
    return values.at[tuple(spot)].set(top_value)


def block_levels(rng, dims, split, least, largest):
    def one(dim, shards_of):
        heights = jax.random.uniform(jax.random.fold_in(jax.random.fold_in(rng, 6), dim), (shards_of,), jnp.float32, least / len(split), largest / len(split))
        return jnp.repeat(jnp.exp(heights), dims[dim] // shards_of).reshape((-1,) + (1,) * (len(dims) - dim - 1))

    loudness = one(*split[0])
    for cut in split[1:]:
        loudness = loudness * one(*cut)
    return loudness


def scatter_about(own_key, dims, deviation, most, cuts=(), dtype=jnp.bfloat16):
    gain = block_levels(own_key, dims, cuts, -0.22, 0.18) if cuts else 1.0
    array = jax.random.normal(own_key, dims, jnp.float32) * deviation * gain
    return jnp.minimum(jnp.maximum(array, -most), most).astype(dtype)


def setup_inputs(seed: int = 0) -> dict:
    splits = jax.random.split(jax.random.key(seed), 4)
    return {
        "rhs": scatter_about(splits[0], (RHS, NX, NY, NZ), 1.0, 6.0, ((1, 256), (2, 4)), jnp.float32),
        "classes": with_ends(jax.random.randint(splits[1], (NX, NY, NZ), 0, 4), jax.random.fold_in(splits[1], 1), 0, 3).astype(jnp.int32),
        "supports": with_ends((jax.random.randint(splits[2], (NX, NY, NZ), 0, 8) < 1).astype(jnp.int32), jax.random.fold_in(splits[2], 1), 0, 1),
    }


SPRING = 8.0
OMEGA = 0.6
DAMP = 0.5
SELF_WEIGHT = 5.0 / 12.0

def stiffness(classes):
    density = (classes.astype(jnp.float32) + 1.0) / 4.0
    return 0.001 + density * density * density

def hex_product(padded, scale_ext):
    nx = scale_ext.shape[0] - 1
    ny = scale_ext.shape[1] - 1
    nz = scale_ext.shape[2] - 1
    corners = {}
    for a in (0, 1):
        for b in (0, 1):
            for c in (0, 1):
                corners[a, b, c] = padded[..., a:a + nx + 1, b:b + ny + 1, c:c + nz + 1]
    summed = sum(corners.values())
    result = None
    for key in corners:
        a, b, c = key
        corner = corners[key]
        adjacent = corners[1 - a, b, c] + corners[a, 1 - b, c] + corners[a, b, 1 - c]
        weighted = scale_ext * (SELF_WEIGHT * corner + adjacent / 12.0 - summed / 12.0)
        piece = weighted[..., 1 - a:1 - a + nx, 1 - b:1 - b + ny, 1 - c:1 - c + nz]
        result = piece if result is None else result + piece
    return result

def prolong(field):
    k, a, b, c = field.shape
    wide = jnp.broadcast_to(field[:, :, None, :, None, :, None], (k, a, 2, b, 2, c, 2))
    return wide.reshape(k, 2 * a, 2 * b, 2 * c)

def restrict(field):
    k, a, b, c = field.shape
    return field.reshape(k, a // 2, 2, b // 2, 2, c // 2, 2).sum(axis=(2, 4, 6))

def inner_block(left, right):
    count = left.shape[0]
    return jnp.dot(left.reshape(count, -1), right.reshape(count, -1).T, precision=lax.Precision.HIGHEST)

def recombine(coef, field):
    count = field.shape[0]
    return jnp.dot(coef.T, field.reshape(count, -1), precision=lax.Precision.HIGHEST).reshape(field.shape)

def spd_solve(matrix, right):
    lower = jnp.linalg.cholesky(matrix)
    middle = lax.linalg.triangular_solve(lower, right, left_side=True, lower=True)
    return lax.linalg.triangular_solve(lower, middle, left_side=True, lower=True, transpose_a=True)

def reference(rhs, classes, supports):
    scale_ext = jnp.pad(stiffness(classes), ((0, 1), (0, 1), (0, 1)))
    support = supports.astype(jnp.float32)
    nx, ny, nz = support.shape
    diagonal = SPRING * support
    for a in (0, 1):
        for b in (0, 1):
            for c in (0, 1):
                diagonal = diagonal + scale_ext[a:a + nx, b:b + ny, c:c + nz] / 3.0
    coarse_step = DAMP / restrict(diagonal[None])[0]

    def apply_one(field):
        padded = jnp.pad(field, ((1, 1), (1, 1), (1, 1)))
        return hex_product(padded, scale_ext) + SPRING * support * field

    def fine_apply(field):
        return lax.map(apply_one, field)

    def precondition(source):
        smoothed = OMEGA * source / diagonal
        coarse_res = restrict(source - fine_apply(smoothed))
        coarse = coarse_step * coarse_res
        for sweep in range(COARSE_SWEEPS):
            coarse = coarse + coarse_step * (coarse_res - restrict(fine_apply(prolong(coarse))))
        smoothed = smoothed + prolong(coarse)
        return smoothed + OMEGA * (source - fine_apply(smoothed)) / diagonal
    first_prec = precondition(rhs)
    applied = fine_apply(first_prec)
    curvature = inner_block(first_prec, applied)
    curvature = 0.5 * (curvature + curvature.T)
    projection = inner_block(first_prec, rhs)
    step_coef = spd_solve(curvature, projection)
    solution = recombine(step_coef, first_prec)
    residual = rhs - recombine(step_coef, applied)
    next_prec = precondition(residual)
    coupling = inner_block(applied, next_prec)
    turn_coef = -spd_solve(curvature, coupling)
    new_direction = next_prec + recombine(turn_coef, first_prec)
    return (solution, residual, new_direction)
```

```python
import jax
import jax.numpy as jnp
from jax import lax
from jax.experimental import pallas as pl
from jax.experimental.pallas import tpu as pltpu
from jax.sharding import Mesh, PartitionSpec as P

SPRING = 8.0
OMEGA = 0.6
DAMP = 0.5
ROWS = 32
LANES = 128
FIELDS = 8
HIGHEST = lax.Precision.HIGHEST
PARAMS = pltpu.CompilerParams(vmem_limit_bytes=24 * 1024 * 1024)


def vmem(n):
    return [pl.BlockSpec(memory_space=pltpu.VMEM)] * n


def iota(axis, shape=(ROWS, LANES)):
    return lax.broadcasted_iota(jnp.int32, shape, axis)


def before_z(v):
    return jnp.where(iota(1) == 0, 0.0, pltpu.roll(v, 1, 1))


def after_z(v):
    return jnp.where(iota(1) == LANES - 1, 0.0, pltpu.roll(v, LANES - 1, 1))


def before_y(v):
    return jnp.where(iota(0) == 0, 0.0, pltpu.roll(v, 1, 0))


def after_y(v):
    return jnp.where(iota(0) == ROWS - 1, 0.0, pltpu.roll(v, ROWS - 1, 0))


def pair_sum(v):
    v = v + jnp.where(iota(0) % 2 == 0, pltpu.roll(v, ROWS - 1, 0), pltpu.roll(v, 1, 0))
    return v + jnp.where(iota(1) % 2 == 0, pltpu.roll(v, LANES - 1, 1), pltpu.roll(v, 1, 1))


def spread(u):
    low = before_z(u)
    out = []
    for f in (u + low, u - low):
        g = before_y(f)
        out += [f + g, f - g]
    return out


def element_plane(lower, upper, s):
    s16, s24, s48 = s * (1.0 / 16.0), s * (1.0 / 24.0), s * (1.0 / 48.0)
    ss, ds, sd, dd = [(b + a, b - a) for a, b in zip(lower, upper)]
    return (
        (None, s16 * ss[1]),
        (s16 * ds[0], s24 * ds[1]),
        (s16 * sd[0], s24 * sd[1]),
        (s24 * dd[0], s48 * dd[1]),
    )


def collect(here, following):
    n = []
    for (s0, d0), (s1, d1) in zip(here, following):
        n.append(d0 - d1 if s0 is None else (s0 + d0) + (s1 - d1))
    ss, ds, sd, dd = n
    ms = (ss + ds) + after_y(ss - ds)
    md = (sd + dd) + after_y(sd - dd)
    return (ms + md) + after_z(ms - md)


def hexes(u, s, least, most, same=lambda p: None):
    gathered, key = None, None
    lower = spread(u(least - 1))
    last, last_id = lower, same(least - 1)
    previous = None
    for e in range(least, most + 2):
        now_id = same(e)
        now = last if now_id is not None and now_id == last_id else spread(u(e))
        w = element_plane(last, now, s(e))
        if previous is not None:
            yield e - 1, collect(previous, w)
        previous, last, last_id = w, now, now_id


class Planes:
    def __init__(self, ref, first):
        self.ref, self.first = ref, first

    def __call__(self, p):
        return self.ref[p - self.first]

    def put(self, p, v):
        self.ref[p - self.first] = v


def from_blocks(refs, field):
    def get(p):
        ref, q = refs[p // 4 + 2], p % 4
        tiles = [ref[x * 2 + q // 2, field, q % 2] for x in range(4)]
        return jnp.concatenate(tiles, axis=0)

    return get


def setup(present, stiff, support, dv, steps):
    sums = None
    diagonal = {}
    for p in range(-7, 12):
        t = stiff(p)
        t = t + after_z(t)
        t = t + after_y(t)
        if sums is not None:
            d = SPRING * support(p - 1) + (sums + t) * (1.0 / 3.0)
            ok = present[(p - 1) // 4 + 2] != 0
            dv.put(p - 1, jnp.where(ok, OMEGA / d, 0.0))
            if (p - 1) % 2 and p - 1 > -7:
                steps.put((p - 1) // 2, jnp.where(ok, DAMP / pair_sum(kept + d), 0.0))
            kept = d
        sums = t


def precondition(source, stiff, support, dv, steps, z, res, c, c1, least, most, emit):
    for p in range(-7, 11):
        z.put(p, dv(p) * source(p))

    def rest(u, lo, hi, same=lambda p: None):
        for p, h in hexes(u, stiff, lo, hi, same):
            yield p, h + SPRING * support(p) * u(p)

    kept = None
    for p, a in rest(z, -6, 9):
        v = source(p) - a
        if p % 2:
            i = p // 2
            r = pair_sum(kept + v)
            res.put(i, r)
            c.put(i, steps(i) * r)
        kept = v

    def sweep(old, new, lo, hi):
        held = None
        for p, a in rest(lambda q: old(q // 2), 2 * lo, 2 * hi + 1, lambda q: q // 2):
            if p % 2:
                i = p // 2
                new.put(i, old(i) + steps(i) * (res(i) - pair_sum(held + a)))
            held = a

    sweep(c, c1, -2, 3)
    sweep(c1, c, -1, 2)
    for p in range(least - 1, most + 2):
        z.put(p, z(p) + c(p // 2))
    for p, a in rest(z, least, most):
        emit(p, z(p) + dv(p) * (source(p) - a))


def store_block(ref, field, q, v):
    for x in range(4):
        tile = v[8 * x : 8 * x + 8]
        if field is None:
            ref[x * 2 + q // 2, q % 2] = tile
        else:
            ref[x * 2 + q // 2, field, q % 2] = tile


def scratch():
    plane = lambda n: pltpu.VMEM((n, ROWS, LANES), jnp.float32)
    return [plane(18), plane(8), plane(18), plane(8), plane(8), plane(8), plane(6)]


def wrap_scratch(dv, steps, z, res, c, c1, out):
    return Planes(dv, -7), Planes(steps, -3), Planes(z, -7), Planes(res, -3), Planes(c, -3), Planes(c1, -3), Planes(out, -1)


def pack_kernel(rhs, classes, supports, out):
    density = (classes[...].astype(jnp.float32) + 1.0) / 4.0
    stiff = 0.001 + density * density * density
    support = supports[...].astype(jnp.float32)
    for j in range(FIELDS):
        out[j, 0] = rhs[j]
        out[j, 1] = stiff
        out[j, 2] = support


def first_kernel(present, m2, m1, own, p1, p2, first, applied, *work):
    refs = (m2, m1, own, p1, p2)
    source, stiff, support = (from_blocks(refs, f) for f in range(3))
    dv, steps, z, res, c, c1, out = wrap_scratch(*work)
    setup(present, stiff, support, dv, steps)

    def emit(p, v):
        out.put(p, v)
        if 0 <= p < 4:
            store_block(first, None, p, v)

    precondition(source, stiff, support, dv, steps, z, res, c, c1, -1, 4, emit)
    for p, h in hexes(out, stiff, 0, 3):
        store_block(applied, None, p, h + SPRING * support(p) * out(p))


def second_kernel(present, m2, m1, own, p1, p2, a_m2, a_m1, a_own, a_p1, a_p2, first, packed, *work):
    refs = (m2, m1, own, p1, p2)
    moved = (a_m2, a_m1, a_own, a_p1, a_p2)
    stiff, support = (from_blocks(refs, f) for f in (1, 2))

    def source(p):
        ref, q = moved[p // 4 + 2], p % 4
        return jnp.concatenate([ref[x * 2 + q // 2, q % 2] for x in range(4)], axis=0)

    dv, steps, z, res, c, c1, _ = wrap_scratch(*work)
    setup(present, stiff, support, dv, steps)
    for p in range(8):
        packed[p, 0] = first[p]
        packed[p, 1] = a_own[p]
    emit = lambda p, v: store_block(packed, 2, p, v)
    precondition(source, stiff, support, dv, steps, z, res, c, c1, 0, 3, emit)


def rows_of(ref, field, fields):
    return jnp.concatenate(
        [ref[pl.ds(field * 16 + t, FIELDS, stride=fields * 16), :] for t in range(16)], axis=1
    )


def gram_kernel(parts, rhs, out):
    f, a, n = (rows_of(parts, k, 3) for k in range(3))
    r = rows_of(rhs, 0, 1)
    left = jnp.concatenate([f, a], axis=0)
    right = jnp.concatenate([a, r, n, f, jnp.zeros((LANES - 32, 2048), jnp.float32)], axis=0)
    g = lax.dot_general(left, right, (((1,), (1,)), ((), ())), precision=HIGHEST, preferred_element_type=jnp.float32)
    tile = jnp.where(iota(1, (8, LANES)) < 16, g[:8], g[8:])
    for k in range(out.shape[0]):
        out[k] = tile


def final_kernel(sums, parts, rhs, sol, resid, direction):
    w = sums[0]
    for k in range(1, sums.shape[0]):
        w = w + sums[k]
    shape = (8, LANES)
    lane, row = iota(1, shape), iota(0, shape)
    w = jnp.where(lane < 8, 0.5 * (w + pltpu.roll(w, LANES - 24, 1)), w)
    for k in range(8):
        pivot = w[k : k + 1, :] / w[k : k + 1, k : k + 1]
        w = jnp.where(row == k, pivot, w - w[:, k : k + 1] * pivot)
    coef = jnp.where((lane >= 8) & (lane < 16), w, 0.0)
    turn = -pltpu.roll(w, LANES - 16, 1)
    for k in range(8):
        turn = turn + w[:, 16 + k : 17 + k] * coef[k : k + 1, :]
    turn = jnp.where((lane >= 8) & (lane < 16), turn, 0.0)
    weights = jnp.concatenate(
        [pltpu.roll(coef, LANES - 8, 1) + pltpu.roll(turn, 8, 1), -coef, -pltpu.roll(coef, 8, 1)], axis=0
    )
    f, a, n = (rows_of(parts, k, 3) for k in range(3))
    fields = jnp.concatenate([f, a, n], axis=0)
    new = lax.dot_general(weights, fields, (((0,), (0,)), ((), ())), precision=HIGHEST, preferred_element_type=jnp.float32)
    r = rows_of(rhs, 0, 1)
    for ref, v in ((sol, new[:8]), (resid, r + new[8:16]), (direction, f + new[16:24])):
        for t in range(16):
            ref[pl.ds(t, FIELDS, stride=16), :] = v[:, LANES * t : LANES * t + LANES]


def f32(*shape):
    return jax.ShapeDtypeStruct(shape, jnp.float32)


def shared_sum(tile, axis):
    return lax.all_to_all(tile, axis, 0, 0)


def local(rhs, classes, supports):
    sizes = {a: lax.axis_size(a) for a in ("z", "y", "c", "x")}
    chips = sizes["z"] * sizes["y"]
    chip = lax.axis_index("z") * sizes["y"] + lax.axis_index("y")
    place = chip + jnp.arange(-2, 3, dtype=jnp.int32)
    present = ((place >= 0) & (place < chips)).astype(jnp.int32)
    smem = [pl.BlockSpec(memory_space=pltpu.SMEM)]

    packed = pl.pallas_call(
        pack_kernel, out_shape=f32(8, 3, 2, 8, LANES), in_specs=vmem(3), out_specs=vmem(1)[0], compiler_params=PARAMS
    )(rhs, classes, supports)
    own = lax.all_to_all(packed, ("x", "c"), 0, 0)

    def around(v):
        def moved(by):
            pairs = [(i, i + by) for i in range(chips) if 0 <= i + by < chips]
            return lax.ppermute(v, ("z", "y"), pairs)

        m1, p1, m2, p2 = moved(1), moved(-1), moved(2), moved(-2)
        return m2, m1, v, p1, p2

    grids = around(own)
    first, applied = pl.pallas_call(
        first_kernel,
        out_shape=(f32(8, 2, 8, LANES), f32(8, 2, 8, LANES)),
        in_specs=smem + vmem(5),
        out_specs=tuple(vmem(2)),
        scratch_shapes=scratch(),
        compiler_params=PARAMS,
    )(present, *grids)
    results = pl.pallas_call(
        second_kernel,
        out_shape=f32(8, 3, 2, 8, LANES),
        in_specs=smem + vmem(11),
        out_specs=vmem(1)[0],
        scratch_shapes=scratch(),
        compiler_params=PARAMS,
    )(present, *grids, *around(applied), first)
    parts = lax.all_to_all(results, ("x", "c"), 0, 0).reshape(8 * 48, LANES)
    rows = rhs.reshape(8 * 16, LANES)

    tile = pl.pallas_call(
        gram_kernel, out_shape=f32(sizes["x"], 8, LANES), in_specs=vmem(2), out_specs=vmem(1)[0], compiler_params=PARAMS
    )(parts, rows)
    tile = shared_sum(tile, "x").sum(0)
    tile = jnp.broadcast_to(tile, (sizes["y"] * sizes["c"], 8, LANES))
    tile = shared_sum(tile, ("y", "c")).sum(0)
    tile = jnp.broadcast_to(tile, (sizes["z"], 8, LANES))
    tile = shared_sum(tile, "z")
    outs = pl.pallas_call(
        final_kernel,
        out_shape=(f32(128, LANES),) * 3,
        in_specs=vmem(3),
        out_specs=tuple(vmem(3)),
        compiler_params=PARAMS,
    )(tile, parts, rows)
    return tuple(v.reshape(8, 2, 8, LANES) for v in outs)


def solution(mesh):
    gx, gy = mesh.shape["gx"], mesh.shape["gy"]
    y = min(8, gx // 2)
    fine = Mesh(mesh.devices.reshape(gx // (2 * y), y, 2, gy), ("z", "y", "c", "x"))
    grid = P(("z", "y", "c"), "x", None)
    fields = P(None, ("z", "y", "c"), "x", None)
    return jax.shard_map(
        local, mesh=fine, in_specs=(fields, grid, grid), out_specs=(fields,) * 3, check_vma=False
    )
```

```python
import jax
import jax.numpy as jnp
from jax import lax
from jax.experimental import pallas as pl
from jax.experimental.pallas import tpu as pltpu
from jax.sharding import Mesh, PartitionSpec as P

SPRING = 8.0
OMEGA = 0.6
DAMP = 0.5
LANES = 128
FIELDS = 8
TILE = (4, 8, LANES)
HIGHEST = lax.Precision.HIGHEST
PARAMS = pltpu.CompilerParams(vmem_limit_bytes=24 * 1024 * 1024)


def vmem(n):
    return [pl.BlockSpec(memory_space=pltpu.VMEM)] * n


def smem():
    return [pl.BlockSpec(memory_space=pltpu.SMEM)]


def iota(axis, shape=TILE):
    return lax.broadcasted_iota(jnp.int32, shape, axis)


def before_z(v):
    return jnp.where(iota(2) == 0, 0.0, pltpu.roll(v, 1, 2))


def after_z(v):
    return jnp.where(iota(2) == LANES - 1, 0.0, pltpu.roll(v, LANES - 1, 2))


def before_y(v):
    r = pltpu.roll(v, 1, 1)
    return jnp.where(iota(1) == 0, jnp.concatenate([jnp.zeros_like(r[:1]), r[:3]], axis=0), r)


def after_y(v):
    r = pltpu.roll(v, 7, 1)
    return jnp.where(iota(1) == 7, jnp.concatenate([r[1:], jnp.zeros_like(r[:1])], axis=0), r)


def pair_sum(v):
    v = v + jnp.where(iota(1) % 2 == 0, pltpu.roll(v, 7, 1), pltpu.roll(v, 1, 1))
    return v + jnp.where(iota(2) % 2 == 0, pltpu.roll(v, LANES - 1, 2), pltpu.roll(v, 1, 2))


def spread(u):
    low = before_z(u)
    out = []
    for f in (u + low, u - low):
        g = before_y(f)
        out += [f + g, f - g]
    return out


def element_plane(lower, upper, s16):
    s24, s48 = s16 * (2.0 / 3.0), s16 * (1.0 / 3.0)
    ss, ds, sd, dd = [(b + a, b - a) for a, b in zip(lower, upper)]
    w = ((s16 * ds[0], s24 * ds[1]), (s16 * sd[0], s24 * sd[1]), (s24 * dd[0], s48 * dd[1]))
    v = s16 * ss[1]
    return [-v] + [a - b for a, b in w], [v] + [a + b for a, b in w]


def gather(n):
    ss, ds, sd, dd = n
    ms = (ss + ds) + after_y(ss - ds)
    md = (sd + dd) + after_y(sd - dd)
    return (ms + md) + after_z(ms - md)


def apply_fine(u, s16, sp8, least, most):
    last, above = spread(u(least - 1)), None
    for e in range(least, most + 2):
        now = spread(u(e))
        to_lower, to_upper = element_plane(last, now, s16(e))
        if above is not None:
            yield e - 1, gather([a + b for a, b in zip(above, to_lower)]) + sp8(e - 1) * u(e - 1)
        last, above = now, to_upper


def apply_coarse(c, s16, sp8, least, most):
    last, above = spread(c(least - 1)), None
    for i in range(least, most + 2):
        now = spread(c(i))
        to_lower, to_upper = element_plane(last, now, s16(2 * i))
        if above is not None:
            inner = s16(2 * i - 1) * 4.0
            part = [inner * last[1], inner * last[2], (inner * (2.0 / 3.0)) * last[3]]
            n = [a + b for a, b in zip(above, to_lower)]
            n = [n[0]] + [a + b for a, b in zip(n[1:], part)]
            yield i - 1, pair_sum(gather(n) + (sp8(2 * i - 2) + sp8(2 * i - 1)) * c(i - 1))
        last, above = now, to_upper


class Planes:
    def __init__(self, ref, first, offset=None):
        self.ref, self.first, self.offset = ref, first, offset

    def at(self, p):
        return p - self.first if self.offset is None else p - self.first + self.offset

    def __call__(self, p):
        return self.ref[self.at(p)]

    def put(self, p, v):
        self.ref[self.at(p)] = v


def precondition(source, s16, sp8, dv, steps, work, least, most, emit):
    z, res, c, c1 = work
    lo, hi = (least - 1) // 2, (most + 1) // 2
    for p in range(2 * lo - 5, 2 * hi + 7):
        z.put(p, dv(p) * source(p))
    kept = None
    for p, a in apply_fine(z, s16, sp8, 2 * lo - 4, 2 * hi + 5):
        v = source(p) - a
        if p % 2:
            i = p // 2
            r = pair_sum(kept + v)
            res.put(i, r)
            c.put(i, steps(i) * r)
        kept = v
    for old, new, first, last in ((c, c1, lo - 1, hi + 1), (c1, c, lo, hi)):
        for i, a in apply_coarse(old, s16, sp8, first, last):
            new.put(i, old(i) + steps(i) * (res(i) - a))
    for p in range(least - 1, most + 2):
        z.put(p, z(p) + c(p // 2))
    for p, a in apply_fine(z, s16, sp8, least, most):
        emit(p, z(p) + dv(p) * (source(p) - a))


def work_shapes():
    plane = lambda n: pltpu.VMEM((n, *TILE), jnp.float32)
    return [plane(24), plane(12), plane(12), plane(12)]


def work_of(z, res, c, c1):
    return Planes(z, -8), Planes(res, -4), Planes(c, -4), Planes(c1, -4)


def pack_kernel(rhs, classes, supports, out, r, k, s, sems):
    copies = [pltpu.make_async_copy(a, b, sems.at[i]) for i, (a, b) in enumerate(((classes, k), (supports, s), (rhs, r)))]
    for copy in copies:
        copy.start()
    copies[0].wait()
    density = (k[...].astype(jnp.float32) + 1.0) / 4.0
    stiff = 0.001 + density * density * density
    for j in range(16):
        out[j, 1] = stiff
    copies[1].wait()
    support = s[...].astype(jnp.float32)
    for j in range(16):
        out[j, 2] = support
    copies[2].wait()
    for x in range(4):
        for c in range(2):
            v = r[x * 2 + c]
            for h in range(2):
                out[(x * 2 + h) * 2 + c, 0] = v


def first_kernel(where, own, swap, far, first, applied, s16_out, sp8_out, dv_out, steps_out, out, source_ref, *work):
    upper_chip = where[0] != 0

    def block(ref, field, q):
        h, c = q // 4, (q // 2) % 2
        return jnp.stack([ref[(x * 2 + h) * 2 + c, field, q % 2] for x in range(4)])

    def plane(field, p):
        q = p % 8
        if 0 <= p < 8:
            return block(own, field, q)
        a, b = block(swap, field, q), block(far, field, q)
        return jnp.where(upper_chip, b, a) if p < 0 else jnp.where(upper_chip, a, b)

    source, s16, sp8, dv = (Planes(r, -8) for r in (source_ref, s16_out, sp8_out, dv_out))
    steps, fields = Planes(steps_out, -4), Planes(out, -1)
    for p in range(-7, 15):
        source.put(p, plane(0, p))
        sp8.put(p, SPRING * plane(2, p))
    sums = kept = None
    for p in range(-7, 16):
        t = plane(1, p)
        s16.put(p, t * (1.0 / 16.0))
        t = t + after_z(t)
        t = t + after_y(t)
        if sums is not None:
            n = p - 1
            d = sp8(n) + (sums + t) * (1.0 / 3.0)
            ok = where[1 + (n + 8) // 8] != 0
            dv.put(n, jnp.where(ok, OMEGA / d, 0.0))
            if n % 2 and n > -7:
                steps.put(n // 2, jnp.where(ok, DAMP / pair_sum(kept + d), 0.0))
            kept = d
        sums = t

    def emit(p, v):
        fields.put(p, v)
        if 0 <= p < 8:
            first[p] = v

    precondition(source, s16, sp8, dv, steps, work_of(*work), -1, 8, emit)
    for p, v in apply_fine(fields, s16, sp8, 0, 7):
        applied[p] = v


def second_kernel(where, first, applied, below, above, s16_ref, sp8_ref, dv_ref, steps_ref, packed, source_ref, *work):
    shift = where[0] * 4
    for q in range(8):
        source_ref[q] = below[q]
        source_ref[8 + q] = applied[q]
        source_ref[16 + q] = above[q]
    source, s16, sp8, dv = (Planes(r, -8, shift) for r in (source_ref, s16_ref, sp8_ref, dv_ref))
    steps = Planes(steps_ref, -4, where[0] * 2)

    def put(field, p, v):
        for x in range(4):
            packed[x * 2 + p // 2, field, p % 2] = v[x]

    for p in range(4):
        put(0, p, first[shift + p])
        put(1, p, applied[shift + p])
    precondition(source, s16, sp8, dv, steps, work_of(*work), 0, 3, lambda p, v: put(2, p, v))


def rows_of(ref, field, fields):
    return jnp.concatenate(
        [ref[pl.ds(field * 16 + t, FIELDS, stride=fields * 16), :] for t in range(16)], axis=1
    )


def gram_kernel(parts, rhs, out):
    f, a, n = (rows_of(parts, k, 3) for k in range(3))
    r = rows_of(rhs, 0, 1)
    left = jnp.concatenate([f, a], axis=0)
    right = jnp.concatenate([a, r, n, f, jnp.zeros((LANES - 32, 2048), jnp.float32)], axis=0)
    g = lax.dot_general(left, right, (((1,), (1,)), ((), ())), precision=HIGHEST, preferred_element_type=jnp.float32)
    tile = jnp.where(iota(1, (8, LANES)) < 16, g[:8], g[8:])
    for k in range(out.shape[0]):
        out[k] = tile


def final_kernel(sums, parts, rhs, sol, resid, direction):
    w = sums[0]
    for k in range(1, sums.shape[0]):
        w = w + sums[k]
    shape = (8, LANES)
    lane, row = iota(1, shape), iota(0, shape)
    w = jnp.where(lane < 8, 0.5 * (w + pltpu.roll(w, LANES - 24, 1)), w)
    for k in range(8):
        pivot = w[k : k + 1, :] / w[k : k + 1, k : k + 1]
        w = jnp.where(row == k, pivot, w - w[:, k : k + 1] * pivot)
    coef = jnp.where((lane >= 8) & (lane < 16), w, 0.0)
    turn = -pltpu.roll(w, LANES - 16, 1)
    for k in range(8):
        turn = turn + w[:, 16 + k : 17 + k] * coef[k : k + 1, :]
    turn = jnp.where((lane >= 8) & (lane < 16), turn, 0.0)
    weights = jnp.concatenate(
        [pltpu.roll(coef, LANES - 8, 1) + pltpu.roll(turn, 8, 1), -coef, -pltpu.roll(coef, 8, 1)], axis=0
    )[:, :24]
    f, a, n = (rows_of(parts, k, 3) for k in range(3))
    fields = jnp.concatenate([f, a, n], axis=0)
    new = lax.dot_general(weights, fields, (((0,), (0,)), ((), ())), precision=HIGHEST, preferred_element_type=jnp.float32)
    r = rows_of(rhs, 0, 1)
    for ref, v in ((sol, new[:8]), (resid, r + new[8:16]), (direction, f + new[16:24])):
        for t in range(16):
            ref[pl.ds(t, FIELDS, stride=16), :] = v[:, LANES * t : LANES * t + LANES]


def f32(*shape):
    return jax.ShapeDtypeStruct(shape, jnp.float32)


def local(rhs, classes, supports):
    sizes = {a: lax.axis_size(a) for a in ("z", "p", "h", "c", "x")}
    chips = sizes["z"] * sizes["p"] * 2
    upper_chip = lax.axis_index("h")
    pair = lax.axis_index("z") * sizes["p"] + lax.axis_index("p") + jnp.arange(-1, 2, dtype=jnp.int32)
    present = ((pair >= 0) & (pair < chips // 2)).astype(jnp.int32)
    where = jnp.concatenate([upper_chip[None].astype(jnp.int32), present])
    chip = ("z", "p", "h")

    packed = pl.pallas_call(
        pack_kernel,
        out_shape=f32(16, 3, 2, 8, LANES),
        in_specs=[pl.BlockSpec(memory_space=pltpu.HBM)] * 3,
        out_specs=vmem(1)[0],
        scratch_shapes=[
            pltpu.VMEM((8, 2, 8, LANES), jnp.float32),
            pltpu.VMEM((2, 8, LANES), jnp.int32),
            pltpu.VMEM((2, 8, LANES), jnp.int32),
            pltpu.SemaphoreType.DMA((3,)),
        ],
        compiler_params=PARAMS,
    )(rhs, classes, supports)
    own = lax.all_to_all(packed, ("x", "h", "c"), 0, 0)

    def moved(v, sources):
        return lax.ppermute(v, chip, [(s, i) for i, s in enumerate(sources) if 0 <= s < chips])

    far = moved(own, [i + 2 if i % 2 == 0 else i - 2 for i in range(chips)])
    swap = moved(own, [i - 1 if i % 2 == 0 else i + 1 for i in range(chips)])
    first, applied, *coefs = pl.pallas_call(
        first_kernel,
        out_shape=[f32(8, *TILE)] * 2 + [f32(24, *TILE)] * 3 + [f32(12, *TILE)],
        in_specs=smem() + vmem(3),
        out_specs=vmem(6),
        scratch_shapes=[pltpu.VMEM((10, *TILE), jnp.float32), pltpu.VMEM((24, *TILE), jnp.float32)] + work_shapes(),
        compiler_params=PARAMS,
    )(where, own, swap, far)
    below = moved(applied, [i - 2 for i in range(chips)])
    above = moved(applied, [i + 2 for i in range(chips)])
    results = pl.pallas_call(
        second_kernel,
        out_shape=f32(8, 3, 2, 8, LANES),
        in_specs=smem() + vmem(8),
        out_specs=vmem(1)[0],
        scratch_shapes=[pltpu.VMEM((24, *TILE), jnp.float32)] + work_shapes(),
        compiler_params=PARAMS,
    )(where, first, applied, below, above, *coefs)
    parts = lax.all_to_all(results, ("x", "c"), 0, 0).reshape(8 * 48, LANES)
    rows = rhs.reshape(8 * 16, LANES)

    tile = pl.pallas_call(
        gram_kernel, out_shape=f32(sizes["x"], 8, LANES), in_specs=vmem(2), out_specs=vmem(1)[0], compiler_params=PARAMS
    )(parts, rows)
    tile = lax.all_to_all(tile, "x", 0, 0).sum(0)
    tile = jnp.broadcast_to(tile, (sizes["p"] * 4, 8, LANES))
    tile = lax.all_to_all(tile, ("p", "h", "c"), 0, 0).sum(0)
    tile = jnp.broadcast_to(tile, (sizes["z"], 8, LANES))
    tile = lax.all_to_all(tile, "z", 0, 0)
    outs = pl.pallas_call(
        final_kernel,
        out_shape=[f32(128, LANES)] * 3,
        in_specs=vmem(3),
        out_specs=vmem(3),
        compiler_params=PARAMS,
    )(tile, parts, rows)
    return tuple(v.reshape(8, 2, 8, LANES) for v in outs)


def solution(mesh):
    gx, gy = mesh.shape["gx"], mesh.shape["gy"]
    y = min(8, gx // 2)
    fine = Mesh(mesh.devices.reshape(gx // (2 * y), y // 2, 2, 2, gy), ("z", "p", "h", "c", "x"))
    across = ("z", "p", "h", "c")
    grid = P(across, "x", None)
    fields = P(None, across, "x", None)
    return jax.shard_map(
        local, mesh=fine, in_specs=(fields, grid, grid), out_specs=(fields,) * 3, check_vma=False
    )
```

```python
import jax
import jax.numpy as jnp
from jax import lax
from jax.experimental import pallas as pl
from jax.experimental.pallas import tpu as pltpu
from jax.sharding import Mesh, PartitionSpec as P

SPRING = 8.0
OMEGA = 0.6
DAMP = 0.5
LANES = 128
FIELDS = 8
TILE = (4, 8, LANES)
HIGHEST = lax.Precision.HIGHEST
PARAMS = pltpu.CompilerParams(vmem_limit_bytes=24 * 1024 * 1024)
WIDE = pltpu.CompilerParams(vmem_limit_bytes=62 * 1024 * 1024)


def vmem(n):
    return [pl.BlockSpec(memory_space=pltpu.VMEM)] * n


def smem():
    return [pl.BlockSpec(memory_space=pltpu.SMEM)]


def iota(axis, shape=TILE):
    return lax.broadcasted_iota(jnp.int32, shape, axis)


def before_z(v):
    return jnp.where(iota(2) == 0, 0.0, pltpu.roll(v, 1, 2))


def after_z(v):
    return jnp.where(iota(2) == LANES - 1, 0.0, pltpu.roll(v, LANES - 1, 2))


def before_y(v):
    r = pltpu.roll(v, 1, 1)
    return jnp.where(iota(1) == 0, jnp.concatenate([jnp.zeros_like(r[:1]), r[:3]], axis=0), r)


def after_y(v):
    r = pltpu.roll(v, 7, 1)
    return jnp.where(iota(1) == 7, jnp.concatenate([r[1:], jnp.zeros_like(r[:1])], axis=0), r)


def pair_sum(v):
    v = v + jnp.where(iota(1) % 2 == 0, pltpu.roll(v, 7, 1), pltpu.roll(v, 1, 1))
    return v + jnp.where(iota(2) % 2 == 0, pltpu.roll(v, LANES - 1, 2), pltpu.roll(v, 1, 2))


def spread(u):
    low = before_z(u)
    out = []
    for f in (u + low, u - low):
        g = before_y(f)
        out += [f + g, f - g]
    return out


def element_plane(lower, upper, s16):
    s24, s48 = s16 * (2.0 / 3.0), s16 * (1.0 / 3.0)
    ss, ds, sd, dd = [(b + a, b - a) for a, b in zip(lower, upper)]
    w = ((s16 * ds[0], s24 * ds[1]), (s16 * sd[0], s24 * sd[1]), (s24 * dd[0], s48 * dd[1]))
    v = s16 * ss[1]
    return [-v] + [a - b for a, b in w], [v] + [a + b for a, b in w]


def gather(n):
    ss, ds, sd, dd = n
    ms = (ss + ds) + after_y(ss - ds)
    md = (sd + dd) + after_y(sd - dd)
    return (ms + md) + after_z(ms - md)


def apply_fine(u, s16, sp8, least, most):
    last, above = spread(u(least - 1)), None
    for e in range(least, most + 2):
        now = spread(u(e))
        to_lower, to_upper = element_plane(last, now, s16(e))
        if above is not None:
            yield e - 1, gather([a + b for a, b in zip(above, to_lower)]) + sp8(e - 1) * u(e - 1)
        last, above = now, to_upper


def apply_coarse(c, s16, sp8, least, most):
    last, above = spread(c(least - 1)), None
    for i in range(least, most + 2):
        now = spread(c(i))
        to_lower, to_upper = element_plane(last, now, s16(2 * i))
        if above is not None:
            inner = s16(2 * i - 1) * 4.0
            part = [inner * last[1], inner * last[2], (inner * (2.0 / 3.0)) * last[3]]
            n = [a + b for a, b in zip(above, to_lower)]
            n = [n[0]] + [a + b for a, b in zip(n[1:], part)]
            yield i - 1, pair_sum(gather(n) + (sp8(2 * i - 2) + sp8(2 * i - 1)) * c(i - 1))
        last, above = now, to_upper


class Planes:
    def __init__(self, ref, first, offset=None):
        self.ref, self.first, self.offset = ref, first, offset

    def at(self, p):
        return p - self.first if self.offset is None else p - self.first + self.offset

    def __call__(self, p):
        return self.ref[self.at(p)]

    def put(self, p, v):
        self.ref[self.at(p)] = v


def precondition(source, s16, sp8, dv, steps, work, least, most, emit):
    z, res, c, c1 = work
    lo, hi = (least - 1) // 2, (most + 1) // 2
    for p in range(2 * lo - 5, 2 * hi + 7):
        z.put(p, dv(p) * source(p))
    kept = None
    for p, a in apply_fine(z, s16, sp8, 2 * lo - 4, 2 * hi + 5):
        v = source(p) - a
        if p % 2:
            i = p // 2
            r = pair_sum(kept + v)
            res.put(i, r)
            c.put(i, steps(i) * r)
        kept = v
    for old, new, first, last in ((c, c1, lo - 1, hi + 1), (c1, c, lo, hi)):
        for i, a in apply_coarse(old, s16, sp8, first, last):
            new.put(i, old(i) + steps(i) * (res(i) - a))
    for p in range(least - 1, most + 2):
        z.put(p, z(p) + c(p // 2))
    for p, a in apply_fine(z, s16, sp8, least, most):
        emit(p, z(p) + dv(p) * (source(p) - a))


def work_shapes():
    plane = lambda n: pltpu.VMEM((n, *TILE), jnp.float32)
    return [plane(24), plane(12), plane(12), plane(12)]


def work_of(z, res, c, c1):
    return Planes(z, -8), Planes(res, -4), Planes(c, -4), Planes(c1, -4)


def pack_kernel(rhs, classes, supports, out, r, k, s, sems):
    copies = [pltpu.make_async_copy(a, b, sems.at[i]) for i, (a, b) in enumerate(((classes, k), (supports, s), (rhs, r)))]
    for copy in copies:
        copy.start()
    copies[0].wait()
    density = (k[...].astype(jnp.float32) + 1.0) / 4.0
    stiff = 0.001 + density * density * density
    for j in range(16):
        out[j, 1] = stiff
    copies[1].wait()
    support = s[...].astype(jnp.float32)
    for j in range(16):
        out[j, 2] = support
    copies[2].wait()
    for x in range(4):
        for c in range(2):
            v = r[x * 2 + c]
            for h in range(2):
                out[(x * 2 + h) * 2 + c, 0] = v


def first_kernel(where, own, swap, far, first, applied, s16_out, sp8_out, dv_out, steps_out, out, source_ref, *work):
    upper_chip = where[0] != 0

    def block(ref, field, q):
        h, c = q // 4, (q // 2) % 2
        return jnp.stack([ref[(x * 2 + h) * 2 + c, field, q % 2] for x in range(4)])

    def plane(field, p):
        q = p % 8
        if 0 <= p < 8:
            return block(own, field, q)
        a, b = block(swap, field, q), block(far, field, q)
        return jnp.where(upper_chip, b, a) if p < 0 else jnp.where(upper_chip, a, b)

    source, s16, sp8, dv = (Planes(r, -8) for r in (source_ref, s16_out, sp8_out, dv_out))
    steps, fields = Planes(steps_out, -4), Planes(out, -1)
    for p in range(-7, 15):
        source.put(p, plane(0, p))
        sp8.put(p, SPRING * plane(2, p))
    sums = kept = None
    for p in range(-7, 16):
        t = plane(1, p)
        s16.put(p, t * (1.0 / 16.0))
        t = t + after_z(t)
        t = t + after_y(t)
        if sums is not None:
            n = p - 1
            d = sp8(n) + (sums + t) * (1.0 / 3.0)
            ok = where[1 + (n + 8) // 8] != 0
            dv.put(n, jnp.where(ok, OMEGA / d, 0.0))
            if n % 2 and n > -7:
                steps.put(n // 2, jnp.where(ok, DAMP / pair_sum(kept + d), 0.0))
            kept = d
        sums = t

    def emit(p, v):
        fields.put(p, v)
        if 0 <= p < 8:
            first[p] = v

    precondition(source, s16, sp8, dv, steps, work_of(*work), -1, 8, emit)
    for p, v in apply_fine(fields, s16, sp8, 0, 7):
        applied[p] = v


def second_kernel(where, first, applied, below, above, s16_ref, sp8_ref, dv_ref, steps_ref, packed, source_ref, *work):
    shift = where[0] * 4
    for q in range(8):
        source_ref[q] = below[q]
        source_ref[8 + q] = applied[q]
        source_ref[16 + q] = above[q]
    source, s16, sp8, dv = (Planes(r, -8, shift) for r in (source_ref, s16_ref, sp8_ref, dv_ref))
    steps = Planes(steps_ref, -4, where[0] * 2)

    def put(field, p, v):
        for x in range(4):
            packed[x * 2 + p // 2, field, p % 2] = v[x]

    for p in range(4):
        put(0, p, first[shift + p])
        put(1, p, applied[shift + p])
    precondition(source, s16, sp8, dv, steps, work_of(*work), 0, 3, lambda p, v: put(2, p, v))


def rows_of(ref, field, fields):
    return jnp.concatenate(
        [ref[pl.ds(field * 16 + t, FIELDS, stride=fields * 16), :] for t in range(16)], axis=1
    )


def gram_kernel(parts, rhs, out):
    f, a, n = (rows_of(parts, k, 3) for k in range(3))
    r = rows_of(rhs, 0, 1)
    left = jnp.concatenate([f, a], axis=0)
    right = jnp.concatenate([a, r, n, f, jnp.zeros((LANES - 32, 2048), jnp.float32)], axis=0)
    g = lax.dot_general(left, right, (((1,), (1,)), ((), ())), precision=HIGHEST, preferred_element_type=jnp.float32)
    lane = iota(1, (8, LANES))
    tile = jnp.where(lane < 16, g[:8], jnp.where(lane < 32, g[8:], 0.0))
    turned = [tile] + [pltpu.roll(tile, 32 * m, 1) for m in range(1, 4)]
    short = jnp.concatenate([sum(turned[m][k + m : k + m + 1] for m in range(4)) for k in (0, 4)], axis=0)
    for k in range(out.shape[0]):
        out[k] = short


def final_kernel(sums, parts, rhs, sol, resid, direction):
    w = sums[0]
    for k in range(1, sums.shape[0]):
        w = w + sums[k]
    turned = [w] + [pltpu.roll(w, LANES - 32 * m, 1) for m in range(1, 4)]
    w = jnp.concatenate([turned[m][k : k + 1] for k in range(2) for m in range(4)], axis=0)
    shape = (8, LANES)
    lane, row = iota(1, shape), iota(0, shape)
    w = jnp.where(lane < 8, 0.5 * (w + pltpu.roll(w, LANES - 24, 1)), w)
    for k in range(8):
        pivot = w[k : k + 1, :] / w[k : k + 1, k : k + 1]
        w = jnp.where(row == k, pivot, w - w[:, k : k + 1] * pivot)
    coef = jnp.where((lane >= 8) & (lane < 16), w, 0.0)
    turn = -pltpu.roll(w, LANES - 16, 1)
    for k in range(8):
        turn = turn + w[:, 16 + k : 17 + k] * coef[k : k + 1, :]
    turn = jnp.where((lane >= 8) & (lane < 16), turn, 0.0)
    weights = jnp.concatenate(
        [pltpu.roll(coef, LANES - 8, 1) + pltpu.roll(turn, 8, 1), -coef, -pltpu.roll(coef, 8, 1)], axis=0
    )[:, :24]
    f, a, n = (rows_of(parts, k, 3) for k in range(3))
    fields = jnp.concatenate([f, a, n], axis=0)
    new = lax.dot_general(weights, fields, (((0,), (0,)), ((), ())), precision=HIGHEST, preferred_element_type=jnp.float32)
    r = rows_of(rhs, 0, 1)
    for ref, v in ((sol, new[:8]), (resid, r + new[8:16]), (direction, f + new[16:24])):
        for t in range(16):
            ref[pl.ds(t, FIELDS, stride=16), :] = v[:, LANES * t : LANES * t + LANES]


def f32(*shape):
    return jax.ShapeDtypeStruct(shape, jnp.float32)


def local(rhs, classes, supports):
    sizes = {a: lax.axis_size(a) for a in ("z", "p", "h", "c", "x")}
    chips = sizes["z"] * sizes["p"] * 2
    upper_chip = lax.axis_index("h")
    pair = lax.axis_index("z") * sizes["p"] + lax.axis_index("p") + jnp.arange(-1, 2, dtype=jnp.int32)
    present = ((pair >= 0) & (pair < chips // 2)).astype(jnp.int32)
    where = jnp.concatenate([upper_chip[None].astype(jnp.int32), present])
    chip = ("z", "p", "h")

    packed = pl.pallas_call(
        pack_kernel,
        out_shape=f32(16, 3, 2, 8, LANES),
        in_specs=[pl.BlockSpec(memory_space=pltpu.HBM)] * 3,
        out_specs=vmem(1)[0],
        scratch_shapes=[
            pltpu.VMEM((8, 2, 8, LANES), jnp.float32),
            pltpu.VMEM((2, 8, LANES), jnp.int32),
            pltpu.VMEM((2, 8, LANES), jnp.int32),
            pltpu.SemaphoreType.DMA((3,)),
        ],
        compiler_params=WIDE,
    )(rhs, classes, supports)
    own = lax.all_to_all(packed, ("x", "h", "c"), 0, 0)

    def moved(v, sources):
        return lax.ppermute(v, chip, [(s, i) for i, s in enumerate(sources) if 0 <= s < chips])

    far = moved(own, [i + 2 if i % 2 == 0 else i - 2 for i in range(chips)])
    swap = moved(own, [i - 1 if i % 2 == 0 else i + 1 for i in range(chips)])
    first, applied, *coefs = pl.pallas_call(
        first_kernel,
        out_shape=[f32(8, *TILE)] * 2 + [f32(24, *TILE)] * 3 + [f32(12, *TILE)],
        in_specs=smem() + vmem(3),
        out_specs=vmem(6),
        scratch_shapes=[pltpu.VMEM((10, *TILE), jnp.float32), pltpu.VMEM((24, *TILE), jnp.float32)] + work_shapes(),
        compiler_params=PARAMS,
    )(where, own, swap, far)
    below = moved(applied, [i - 2 for i in range(chips)])
    above = moved(applied, [i + 2 for i in range(chips)])
    results = pl.pallas_call(
        second_kernel,
        out_shape=f32(8, 3, 2, 8, LANES),
        in_specs=smem() + vmem(8),
        out_specs=vmem(1)[0],
        scratch_shapes=[pltpu.VMEM((24, *TILE), jnp.float32)] + work_shapes(),
        compiler_params=PARAMS,
    )(where, first, applied, below, above, *coefs)
    parts = lax.all_to_all(results, ("x", "c"), 0, 0).reshape(8 * 48, LANES)
    rows = rhs.reshape(8 * 16, LANES)

    tile = pl.pallas_call(
        gram_kernel, out_shape=f32(sizes["p"] * 4 * sizes["x"], 2, LANES), in_specs=vmem(2), out_specs=vmem(1)[0], compiler_params=PARAMS
    )(parts, rows)
    tile = lax.all_to_all(tile, ("x", "p", "h", "c"), 0, 0).sum(0)
    tile = jnp.broadcast_to(tile, (sizes["z"], 2, LANES))
    tile = lax.all_to_all(tile, "z", 0, 0)
    outs = pl.pallas_call(
        final_kernel,
        out_shape=[f32(128, LANES)] * 3,
        in_specs=vmem(3),
        out_specs=vmem(3),
        compiler_params=PARAMS,
    )(tile, parts, rows)
    return tuple(v.reshape(8, 2, 8, LANES) for v in outs)


def solution(mesh):
    gx, gy = mesh.shape["gx"], mesh.shape["gy"]
    y = min(8, gx // 2)
    fine = Mesh(mesh.devices.reshape(gx // (2 * y), y // 2, 2, 2, gy), ("z", "p", "h", "c", "x"))
    across = ("z", "p", "h", "c")
    grid = P(across, "x", None)
    fields = P(None, across, "x", None)
    return jax.shard_map(
        local, mesh=fine, in_specs=(fields, grid, grid), out_specs=(fields,) * 3, check_vma=False
    )
```

```python
import jax
import jax.numpy as jnp
from jax import lax
from jax.experimental import pallas as pl
from jax.experimental.pallas import tpu as pltpu
from jax.sharding import Mesh, PartitionSpec as P

SPRING = 8.0
OMEGA = 0.6
DAMP = 0.5
LANES = 128
FIELDS = 8
TILE = (4, 8, LANES)
HIGHEST = lax.Precision.HIGHEST
PARAMS = pltpu.CompilerParams(vmem_limit_bytes=24 * 1024 * 1024)
WIDE = pltpu.CompilerParams(vmem_limit_bytes=62 * 1024 * 1024)


def vmem(n):
    return [pl.BlockSpec(memory_space=pltpu.VMEM)] * n


def smem():
    return [pl.BlockSpec(memory_space=pltpu.SMEM)]


def iota(axis, shape=TILE):
    return lax.broadcasted_iota(jnp.int32, shape, axis)


def before_z(v):
    return jnp.where(iota(2) == 0, 0.0, pltpu.roll(v, 1, 2))


def after_z(v):
    return jnp.where(iota(2) == LANES - 1, 0.0, pltpu.roll(v, LANES - 1, 2))


def before_y(v):
    r = pltpu.roll(v, 1, 1)
    return jnp.where(iota(1) == 0, jnp.concatenate([jnp.zeros_like(r[:1]), r[:3]], axis=0), r)


def after_y(v):
    r = pltpu.roll(v, 7, 1)
    return jnp.where(iota(1) == 7, jnp.concatenate([r[1:], jnp.zeros_like(r[:1])], axis=0), r)


def pair_sum(v):
    v = v + jnp.where(iota(1) % 2 == 0, pltpu.roll(v, 7, 1), pltpu.roll(v, 1, 1))
    return v + jnp.where(iota(2) % 2 == 0, pltpu.roll(v, LANES - 1, 2), pltpu.roll(v, 1, 2))


def spread(u):
    low = before_z(u)
    out = []
    for f in (u + low, u - low):
        g = before_y(f)
        out += [f + g, f - g]
    return out


def element_plane(lower, upper, s16):
    s24, s48 = s16 * (2.0 / 3.0), s16 * (1.0 / 3.0)
    ss, ds, sd, dd = [(b + a, b - a) for a, b in zip(lower, upper)]
    w = ((s16 * ds[0], s24 * ds[1]), (s16 * sd[0], s24 * sd[1]), (s24 * dd[0], s48 * dd[1]))
    v = s16 * ss[1]
    return [-v] + [a - b for a, b in w], [v] + [a + b for a, b in w]


def gather(n):
    ss, ds, sd, dd = n
    ms = (ss + ds) + after_y(ss - ds)
    md = (sd + dd) + after_y(sd - dd)
    return (ms + md) + after_z(ms - md)


def apply_fine(u, s16, sp8, least, most):
    last, above = spread(u(least - 1)), None
    for e in range(least, most + 2):
        now = spread(u(e))
        to_lower, to_upper = element_plane(last, now, s16(e))
        if above is not None:
            yield e - 1, gather([a + b for a, b in zip(above, to_lower)]) + sp8(e - 1) * u(e - 1)
        last, above = now, to_upper


def apply_coarse(c, s16, sp8, least, most):
    last, above = spread(c(least - 1)), None
    for i in range(least, most + 2):
        now = spread(c(i))
        to_lower, to_upper = element_plane(last, now, s16(2 * i))
        if above is not None:
            inner = s16(2 * i - 1) * 4.0
            part = [inner * last[1], inner * last[2], (inner * (2.0 / 3.0)) * last[3]]
            n = [a + b for a, b in zip(above, to_lower)]
            n = [n[0]] + [a + b for a, b in zip(n[1:], part)]
            yield i - 1, pair_sum(gather(n) + (sp8(2 * i - 2) + sp8(2 * i - 1)) * c(i - 1))
        last, above = now, to_upper


class Planes:
    def __init__(self, ref, first, offset=None):
        self.ref, self.first, self.offset = ref, first, offset

    def at(self, p):
        return p - self.first if self.offset is None else p - self.first + self.offset

    def __call__(self, p):
        return self.ref[self.at(p)]

    def put(self, p, v):
        self.ref[self.at(p)] = v


def precondition(source, s16, sp8, dv, steps, work, least, most, emit):
    z, res, c, c1 = work
    lo, hi = (least - 1) // 2, (most + 1) // 2
    for p in range(2 * lo - 5, 2 * hi + 7):
        z.put(p, dv(p) * source(p))
    kept = None
    for p, a in apply_fine(z, s16, sp8, 2 * lo - 4, 2 * hi + 5):
        v = source(p) - a
        if p % 2:
            i = p // 2
            r = pair_sum(kept + v)
            res.put(i, r)
            c.put(i, steps(i) * r)
        kept = v
    for old, new, first, last in ((c, c1, lo - 1, hi + 1), (c1, c, lo, hi)):
        for i, a in apply_coarse(old, s16, sp8, first, last):
            new.put(i, old(i) + steps(i) * (res(i) - a))
    for p in range(least - 1, most + 2):
        z.put(p, z(p) + c(p // 2))
    for p, a in apply_fine(z, s16, sp8, least, most):
        emit(p, z(p) + dv(p) * (source(p) - a))


def work_shapes():
    plane = lambda n: pltpu.VMEM((n, *TILE), jnp.float32)
    return [plane(24), plane(12), plane(12), plane(12)]


def work_of(z, res, c, c1):
    return Planes(z, -8), Planes(res, -4), Planes(c, -4), Planes(c1, -4)


def pack_kernel(rhs, classes, supports, out, r, k, s, sems):
    copies = [pltpu.make_async_copy(a, b, sems.at[i]) for i, (a, b) in enumerate(((classes, k), (supports, s), (rhs, r)))]
    for copy in copies:
        copy.start()
    copies[0].wait()
    density = (k[...].astype(jnp.float32) + 1.0) / 4.0
    stiff = 0.001 + density * density * density
    for j in range(0, 16, 2):
        out[j, 0] = stiff
    copies[1].wait()
    support = s[...].astype(jnp.float32)
    for j in range(1, 16, 2):
        out[j, 0] = support
    copies[2].wait()
    for x in range(4):
        for c in range(2):
            v = r[x * 2 + c]
            for h in range(2):
                out[(x * 2 + h) * 2 + c, 1] = v


def grids_kernel(*refs):
    *blocks, out = refs
    for i, ref in enumerate(blocks):
        for j in range(16):
            out[i, j] = ref[j, 0]


def first_kernel(
    where, own, swap, far, own_other, halo_other, first, applied, s16_out, sp8_out, dv_out, steps_out, out, source_ref, *work
):
    upper_chip, upper_core = where[0] != 0, where[4] != 0

    def block(ref, field, q):
        h, c = q // 4, (q // 2) % 2
        return jnp.stack([ref[(x * 2 + h) * 2 + c, *field, q % 2] for x in range(4)])

    def plane(field, p, other=None):
        q = p % 8
        if 0 <= p < 8:
            return block(own if other is None else own_other.at[0], field, q)
        if other is None:
            a, b = block(swap, field, q), block(far, field, q)
        else:
            a, b = block(halo_other.at[0], field, q), block(halo_other.at[1], field, q)
        return jnp.where(upper_chip, b, a) if p < 0 else jnp.where(upper_chip, a, b)

    def grids(p):
        a, b = plane((0,), p), plane((), p, True)
        return jnp.where(upper_core, b, a), jnp.where(upper_core, a, b)

    source, s16, sp8, dv = (Planes(r, -8) for r in (source_ref, s16_out, sp8_out, dv_out))
    steps, fields = Planes(steps_out, -4), Planes(out, -1)
    for p in range(-7, 15):
        source.put(p, plane((1,), p))
    sums = kept = None
    for p in range(-7, 16):
        t, support = grids(p)
        sp8.put(p, SPRING * support)
        s16.put(p, t * (1.0 / 16.0))
        t = t + after_z(t)
        t = t + after_y(t)
        if sums is not None:
            n = p - 1
            d = sp8(n) + (sums + t) * (1.0 / 3.0)
            ok = where[1 + (n + 8) // 8] != 0
            dv.put(n, jnp.where(ok, OMEGA / d, 0.0))
            if n % 2 and n > -7:
                steps.put(n // 2, jnp.where(ok, DAMP / pair_sum(kept + d), 0.0))
            kept = d
        sums = t

    def emit(p, v):
        fields.put(p, v)
        if 0 <= p < 8:
            first[p] = v

    precondition(source, s16, sp8, dv, steps, work_of(*work), -1, 8, emit)
    for p, v in apply_fine(fields, s16, sp8, 0, 7):
        applied[p] = v


def second_kernel(where, first, applied, below, above, s16_ref, sp8_ref, dv_ref, steps_ref, packed, source_ref, *work):
    shift = where[0] * 4
    for q in range(8):
        source_ref[q] = below[q]
        source_ref[8 + q] = applied[q]
        source_ref[16 + q] = above[q]
    source, s16, sp8, dv = (Planes(r, -8, shift) for r in (source_ref, s16_ref, sp8_ref, dv_ref))
    steps = Planes(steps_ref, -4, where[0] * 2)

    def put(field, p, v):
        for x in range(4):
            packed[x * 2 + p // 2, field, p % 2] = v[x]

    for p in range(4):
        put(0, p, first[shift + p])
        put(1, p, applied[shift + p])
    precondition(source, s16, sp8, dv, steps, work_of(*work), 0, 3, lambda p, v: put(2, p, v))


def rows_of(ref, field, fields):
    return jnp.concatenate(
        [ref[pl.ds(field * 16 + t, FIELDS, stride=fields * 16), :] for t in range(16)], axis=1
    )


def gram_kernel(parts, rhs, out):
    f, a, n = (rows_of(parts, k, 3) for k in range(3))
    r = rows_of(rhs, 0, 1)
    left = jnp.concatenate([f, a], axis=0)
    right = jnp.concatenate([a, r, n, f, jnp.zeros((LANES - 32, 2048), jnp.float32)], axis=0)
    g = lax.dot_general(left, right, (((1,), (1,)), ((), ())), precision=HIGHEST, preferred_element_type=jnp.float32)
    lane = iota(1, (8, LANES))
    tile = jnp.where(lane < 16, g[:8], jnp.where(lane < 32, g[8:], 0.0))
    turned = [tile] + [pltpu.roll(tile, 32 * m, 1) for m in range(1, 4)]
    short = jnp.concatenate([sum(turned[m][k + m : k + m + 1] for m in range(4)) for k in (0, 4)], axis=0)
    for k in range(out.shape[0]):
        out[k] = short


def final_kernel(sums, parts, rhs, sol, resid, direction):
    w = sums[0]
    for k in range(1, sums.shape[0]):
        w = w + sums[k]
    turned = [w] + [pltpu.roll(w, LANES - 32 * m, 1) for m in range(1, 4)]
    w = jnp.concatenate([turned[m][k : k + 1] for k in range(2) for m in range(4)], axis=0)
    shape = (8, LANES)
    lane, row = iota(1, shape), iota(0, shape)
    w = jnp.where(lane < 8, 0.5 * (w + pltpu.roll(w, LANES - 24, 1)), w)
    for k in range(8):
        pivot = w[k : k + 1, :] / w[k : k + 1, k : k + 1]
        w = jnp.where(row == k, pivot, w - w[:, k : k + 1] * pivot)
    coef = jnp.where((lane >= 8) & (lane < 16), w, 0.0)
    turn = -pltpu.roll(w, LANES - 16, 1)
    for k in range(8):
        turn = turn + w[:, 16 + k : 17 + k] * coef[k : k + 1, :]
    turn = jnp.where((lane >= 8) & (lane < 16), turn, 0.0)
    weights = jnp.concatenate(
        [pltpu.roll(coef, LANES - 8, 1) + pltpu.roll(turn, 8, 1), -coef, -pltpu.roll(coef, 8, 1)], axis=0
    )[:, :24]
    f, a, n = (rows_of(parts, k, 3) for k in range(3))
    fields = jnp.concatenate([f, a, n], axis=0)
    new = lax.dot_general(weights, fields, (((0,), (0,)), ((), ())), precision=HIGHEST, preferred_element_type=jnp.float32)
    r = rows_of(rhs, 0, 1)
    for ref, v in ((sol, new[:8]), (resid, r + new[8:16]), (direction, f + new[16:24])):
        for t in range(16):
            ref[pl.ds(t, FIELDS, stride=16), :] = v[:, LANES * t : LANES * t + LANES]


def f32(*shape):
    return jax.ShapeDtypeStruct(shape, jnp.float32)


def local(rhs, classes, supports):
    sizes = {a: lax.axis_size(a) for a in ("z", "p", "h", "c", "x")}
    chips = sizes["z"] * sizes["p"] * 2
    upper_chip = lax.axis_index("h")
    pair = lax.axis_index("z") * sizes["p"] + lax.axis_index("p") + jnp.arange(-1, 2, dtype=jnp.int32)
    present = ((pair >= 0) & (pair < chips // 2)).astype(jnp.int32)
    core = lax.axis_index("c")
    where = jnp.concatenate([upper_chip[None].astype(jnp.int32), present, core[None].astype(jnp.int32)])
    chip = ("z", "p", "h")

    packed = pl.pallas_call(
        pack_kernel,
        out_shape=f32(16, 2, 2, 8, LANES),
        in_specs=[pl.BlockSpec(memory_space=pltpu.HBM)] * 3,
        out_specs=vmem(1)[0],
        scratch_shapes=[
            pltpu.VMEM((8, 2, 8, LANES), jnp.float32),
            pltpu.VMEM((2, 8, LANES), jnp.int32),
            pltpu.VMEM((2, 8, LANES), jnp.int32),
            pltpu.SemaphoreType.DMA((3,)),
        ],
        compiler_params=WIDE,
    )(rhs, classes, supports)
    own = lax.all_to_all(packed, ("x", "h", "c"), 0, 0)

    def moved(v, sources):
        return lax.ppermute(v, chip, [(s, i) for i, s in enumerate(sources) if 0 <= s < chips])

    far = moved(own, [i + 2 if i % 2 == 0 else i - 2 for i in range(chips)])
    swap = moved(own, [i - 1 if i % 2 == 0 else i + 1 for i in range(chips)])

    def partner(*blocks):
        n = len(blocks)
        grids = pl.pallas_call(
            grids_kernel,
            out_shape=f32(n, 16, 2, 8, LANES),
            in_specs=vmem(n),
            out_specs=vmem(1)[0],
            compiler_params=PARAMS,
        )(*blocks)
        return lax.ppermute(grids, "c", [(0, 1), (1, 0)])

    own_other, halo_other = partner(own), partner(swap, far)
    first, applied, *coefs = pl.pallas_call(
        first_kernel,
        out_shape=[f32(8, *TILE)] * 2 + [f32(24, *TILE)] * 3 + [f32(12, *TILE)],
        in_specs=smem() + vmem(5),
        out_specs=vmem(6),
        scratch_shapes=[pltpu.VMEM((10, *TILE), jnp.float32), pltpu.VMEM((24, *TILE), jnp.float32)] + work_shapes(),
        compiler_params=PARAMS,
    )(where, own, swap, far, own_other, halo_other)
    below = moved(applied, [i - 2 for i in range(chips)])
    above = moved(applied, [i + 2 for i in range(chips)])
    results = pl.pallas_call(
        second_kernel,
        out_shape=f32(8, 3, 2, 8, LANES),
        in_specs=smem() + vmem(8),
        out_specs=vmem(1)[0],
        scratch_shapes=[pltpu.VMEM((24, *TILE), jnp.float32)] + work_shapes(),
        compiler_params=PARAMS,
    )(where, first, applied, below, above, *coefs)
    parts = lax.all_to_all(results, ("x", "c"), 0, 0).reshape(8 * 48, LANES)
    rows = rhs.reshape(8 * 16, LANES)

    tile = pl.pallas_call(
        gram_kernel, out_shape=f32(sizes["p"] * 4 * sizes["x"], 2, LANES), in_specs=vmem(2), out_specs=vmem(1)[0], compiler_params=PARAMS
    )(parts, rows)
    tile = lax.all_to_all(tile, ("x", "p", "h", "c"), 0, 0).sum(0)
    tile = jnp.broadcast_to(tile, (sizes["z"], 2, LANES))
    tile = lax.all_to_all(tile, "z", 0, 0)
    outs = pl.pallas_call(
        final_kernel,
        out_shape=[f32(128, LANES)] * 3,
        in_specs=vmem(3),
        out_specs=vmem(3),
        compiler_params=PARAMS,
    )(tile, parts, rows)
    return tuple(v.reshape(8, 2, 8, LANES) for v in outs)


def solution(mesh):
    gx, gy = mesh.shape["gx"], mesh.shape["gy"]
    y = min(8, gx // 2)
    fine = Mesh(mesh.devices.reshape(gx // (2 * y), y // 2, 2, 2, gy), ("z", "p", "h", "c", "x"))
    across = ("z", "p", "h", "c")
    grid = P(across, "x", None)
    fields = P(None, across, "x", None)
    return jax.shard_map(
        local, mesh=fine, in_specs=(fields, grid, grid), out_specs=(fields,) * 3, check_vma=False
    )
```

```python
import jax
import jax.numpy as jnp
from jax import lax
from jax.experimental import pallas as pl
from jax.experimental.pallas import tpu as pltpu
from jax.sharding import Mesh, PartitionSpec as P

SPRING = 8.0
OMEGA = 0.6
DAMP = 0.5
LANES = 128
FIELDS = 8
TILE = (4, 8, LANES)
HIGHEST = lax.Precision.HIGHEST
PARAMS = pltpu.CompilerParams(vmem_limit_bytes=24 * 1024 * 1024)
WIDE = pltpu.CompilerParams(vmem_limit_bytes=62 * 1024 * 1024)


def vmem(n):
    return [pl.BlockSpec(memory_space=pltpu.VMEM)] * n


def smem():
    return [pl.BlockSpec(memory_space=pltpu.SMEM)]


def iota(axis, shape=TILE):
    return lax.broadcasted_iota(jnp.int32, shape, axis)


def before_z(v):
    return jnp.where(iota(2) == 0, 0.0, pltpu.roll(v, 1, 2))


def after_z(v):
    return jnp.where(iota(2) == LANES - 1, 0.0, pltpu.roll(v, LANES - 1, 2))


def before_y(v):
    r = pltpu.roll(v, 1, 1)
    return jnp.where(iota(1) == 0, jnp.concatenate([jnp.zeros_like(r[:1]), r[:3]], axis=0), r)


def after_y(v):
    r = pltpu.roll(v, 7, 1)
    return jnp.where(iota(1) == 7, jnp.concatenate([r[1:], jnp.zeros_like(r[:1])], axis=0), r)


def pair_sum(v):
    v = (v + jnp.where(iota(1) % 2 == 0, pltpu.roll(v, 7, 1), pltpu.roll(v, 1, 1))).reshape(32, LANES)
    square = (LANES, LANES)
    ones = (iota(0, square) // 2 == iota(1, square) // 2).astype(jnp.bfloat16)
    high = v.astype(jnp.bfloat16)
    rest = v - high.astype(jnp.float32)
    middle = rest.astype(jnp.bfloat16)
    low = (rest - middle.astype(jnp.float32)).astype(jnp.bfloat16)
    pieces = jnp.concatenate([high, middle, low], axis=1)
    ones = jnp.concatenate([ones] * 3, axis=0)
    return jnp.dot(pieces, ones, preferred_element_type=jnp.float32).reshape(TILE)


def spread(u):
    low = before_z(u)
    out = []
    for f in (u + low, u - low):
        g = before_y(f)
        out += [f + g, f - g]
    return out


def element_plane(lower, upper, s16):
    s24, s48 = s16 * (2.0 / 3.0), s16 * (1.0 / 3.0)
    ss, ds, sd, dd = [(b + a, b - a) for a, b in zip(lower, upper)]
    w = ((s16 * ds[0], s24 * ds[1]), (s16 * sd[0], s24 * sd[1]), (s24 * dd[0], s48 * dd[1]))
    v = s16 * ss[1]
    return [-v] + [a - b for a, b in w], [v] + [a + b for a, b in w]


def gather(n):
    ss, ds, sd, dd = n
    ms = (ss + ds) + after_y(ss - ds)
    md = (sd + dd) + after_y(sd - dd)
    return (ms + md) + after_z(ms - md)


def apply_fine(u, s16, sp8, least, most):
    last, above = spread(u(least - 1)), None
    for e in range(least, most + 2):
        now = spread(u(e))
        to_lower, to_upper = element_plane(last, now, s16(e))
        if above is not None:
            yield e - 1, gather([a + b for a, b in zip(above, to_lower)]) + sp8(e - 1) * u(e - 1)
        last, above = now, to_upper


def restricted(even, odd, s16, least, most):
    last, above = (even if odd is None else odd)(least - 1), None
    for i in range(least, most + 2):
        now = even(i)
        to_lower, to_upper = element_plane(last, now, s16(2 * i))
        if above is not None:
            n = [a + b for a, b in zip(above, to_lower)]
            yield i - 1, gather([n[0]] + [a + b for a, b in zip(n[1:], inside)])
        if i <= most:
            last = now if odd is None else odd(i)
            inner = s16(2 * i + 1) * (4.0 if odd is None else 2.0)
            both = now if odd is None else [a + b for a, b in zip(now, last)]
            inside = [inner * both[1], inner * both[2], (inner * (2.0 / 3.0)) * both[3]]
        above = to_upper


def apply_coarse(c, s16, sp8, least, most):
    for i, h in restricted(lambda i: spread(c(i)), None, s16, least, most):
        yield i, pair_sum(h + (sp8(2 * i) + sp8(2 * i + 1)) * c(i))


def coarse_residual(source, u, s16, sp8, least, most):
    for i, h in restricted(lambda i: spread(u(2 * i)), lambda i: spread(u(2 * i + 1)), s16, least, most):
        a, b = 2 * i, 2 * i + 1
        yield i, pair_sum((source(a) - sp8(a) * u(a)) + (source(b) - sp8(b) * u(b)) - h)


class Planes:
    def __init__(self, ref, first, offset=None):
        self.ref, self.first, self.offset = ref, first, offset

    def at(self, p):
        return p - self.first if self.offset is None else p - self.first + self.offset

    def __call__(self, p):
        return self.ref[self.at(p)]

    def put(self, p, v):
        self.ref[self.at(p)] = v


def precondition(source, s16, sp8, dv, steps, work, least, most, emit):
    z, res, c, c1 = work
    lo, hi = (least - 1) // 2, (most + 1) // 2
    for p in range(2 * lo - 5, 2 * hi + 7):
        z.put(p, dv(p) * source(p))
    for i, r in coarse_residual(source, z, s16, sp8, lo - 2, hi + 2):
        res.put(i, r)
        c.put(i, steps(i) * r)
    for old, new, first, last in ((c, c1, lo - 1, hi + 1), (c1, c, lo, hi)):
        for i, a in apply_coarse(old, s16, sp8, first, last):
            new.put(i, old(i) + steps(i) * (res(i) - a))
    for p in range(least - 1, most + 2):
        z.put(p, z(p) + c(p // 2))
    for p, a in apply_fine(z, s16, sp8, least, most):
        emit(p, z(p) + dv(p) * (source(p) - a))


def work_shapes():
    plane = lambda n: pltpu.VMEM((n, *TILE), jnp.float32)
    return [plane(24), plane(12), plane(12), plane(12)]


def work_of(z, res, c, c1):
    return Planes(z, -8), Planes(res, -4), Planes(c, -4), Planes(c1, -4)


def pack_kernel(rhs, classes, supports, out, r, k, s, sems):
    copies = [pltpu.make_async_copy(a, b, sems.at[i]) for i, (a, b) in enumerate(((classes, k), (supports, s), (rhs, r)))]
    for copy in copies:
        copy.start()
    copies[0].wait()
    density = (k[...].astype(jnp.float32) + 1.0) / 4.0
    stiff = 0.001 + density * density * density
    for j in range(0, 16, 2):
        out[j, 0] = stiff
    copies[1].wait()
    support = s[...].astype(jnp.float32)
    for j in range(1, 16, 2):
        out[j, 0] = support
    copies[2].wait()
    for x in range(4):
        for c in range(2):
            v = r[x * 2 + c]
            for h in range(2):
                out[(x * 2 + h) * 2 + c, 1] = v


def grids_kernel(*refs):
    *blocks, out = refs
    for i, ref in enumerate(blocks):
        for j in range(16):
            out[i, j] = ref[j, 0]


def first_kernel(
    where, own, swap, far, other, first, applied, s16_out, sp8_out, dv_out, steps_out, out, source_ref, *work
):
    upper_chip, upper_core = where[0] != 0, where[4] != 0

    def block(ref, field, q):
        h, c = q // 4, (q // 2) % 2
        return jnp.stack([ref[(x * 2 + h) * 2 + c, *field, q % 2] for x in range(4)])

    def plane(field, p, grid=None):
        q = p % 8
        if 0 <= p < 8:
            return block(own if grid is None else grid.at[0], field, q)
        a, b = (swap, far) if grid is None else (grid.at[1], grid.at[2])
        a, b = block(a, field, q), block(b, field, q)
        return jnp.where(upper_chip, b, a) if p < 0 else jnp.where(upper_chip, a, b)

    def grids(p):
        a, b = plane((0,), p), plane((), p, other)
        return jnp.where(upper_core, b, a), jnp.where(upper_core, a, b)

    source, s16, sp8, dv = (Planes(r, -8) for r in (source_ref, s16_out, sp8_out, dv_out))
    steps, fields = Planes(steps_out, -4), Planes(out, -1)
    for p in range(-7, 15):
        source.put(p, plane((1,), p))
    sums = kept = None
    for p in range(-7, 16):
        t, support = grids(p)
        sp8.put(p, SPRING * support)
        s16.put(p, t * (1.0 / 16.0))
        t = t + after_z(t)
        t = t + after_y(t)
        if sums is not None:
            n = p - 1
            d = sp8(n) + (sums + t) * (1.0 / 3.0)
            ok = where[1 + (n + 8) // 8] != 0
            dv.put(n, jnp.where(ok, OMEGA / d, 0.0))
            if n % 2 and n > -7:
                steps.put(n // 2, jnp.where(ok, DAMP / pair_sum(kept + d), 0.0))
            kept = d
        sums = t

    def emit(p, v):
        fields.put(p, v)
        if 0 <= p < 8:
            first[p] = v

    precondition(source, s16, sp8, dv, steps, work_of(*work), -1, 8, emit)
    for p, v in apply_fine(fields, s16, sp8, 0, 7):
        applied[p] = v


def second_kernel(where, first, applied, below, above, s16_ref, sp8_ref, dv_ref, steps_ref, packed, source_ref, *work):
    shift = where[0] * 4
    for q in range(8):
        source_ref[q] = below[q]
        source_ref[8 + q] = applied[q]
        source_ref[16 + q] = above[q]
    source, s16, sp8, dv = (Planes(r, -8, shift) for r in (source_ref, s16_ref, sp8_ref, dv_ref))
    steps = Planes(steps_ref, -4, where[0] * 2)

    def put(field, p, v):
        for x in range(4):
            packed[x * 2 + p // 2, field, p % 2] = v[x]

    for p in range(4):
        put(0, p, first[shift + p])
        put(1, p, applied[shift + p])
    precondition(source, s16, sp8, dv, steps, work_of(*work), 0, 3, lambda p, v: put(2, p, v))


def rows_of(ref, field, fields):
    return jnp.concatenate(
        [ref[pl.ds(field * 16 + t, FIELDS, stride=fields * 16), :] for t in range(16)], axis=1
    )


def gram_kernel(parts, rhs, out):
    f, a, n = (rows_of(parts, k, 3) for k in range(3))
    r = rows_of(rhs, 0, 1)
    left = jnp.concatenate([f, a], axis=0)
    right = jnp.concatenate([a, r, n, f, jnp.zeros((LANES - 32, 2048), jnp.float32)], axis=0)
    g = lax.dot_general(left, right, (((1,), (1,)), ((), ())), precision=HIGHEST, preferred_element_type=jnp.float32)
    lane = iota(1, (8, LANES))
    tile = jnp.where(lane < 16, g[:8], jnp.where(lane < 32, g[8:], 0.0))
    turned = [tile] + [pltpu.roll(tile, 32 * m, 1) for m in range(1, 4)]
    short = jnp.concatenate([sum(turned[m][k + m : k + m + 1] for m in range(4)) for k in (0, 4)], axis=0)
    for k in range(out.shape[0]):
        out[k] = short


def final_kernel(sums, parts, rhs, sol, resid, direction):
    w = sums[0]
    for k in range(1, sums.shape[0]):
        w = w + sums[k]
    turned = [w] + [pltpu.roll(w, LANES - 32 * m, 1) for m in range(1, 4)]
    w = jnp.concatenate([turned[m][k : k + 1] for k in range(2) for m in range(4)], axis=0)
    shape = (8, LANES)
    lane, row = iota(1, shape), iota(0, shape)
    w = jnp.where(lane < 8, 0.5 * (w + pltpu.roll(w, LANES - 24, 1)), w)
    scale = jnp.ones(shape, jnp.float32)
    for k in range(8):
        column = jnp.broadcast_to(w[:, k : k + 1], shape)
        inverse = 1.0 / jnp.broadcast_to(column[k : k + 1, :], shape)
        scale = jnp.where(row == k, inverse, scale)
        w = w - jnp.where(row == k, 0.0, column * inverse) * w[k : k + 1, :]
    w = w * scale
    coef = jnp.where((lane >= 8) & (lane < 16), w, 0.0)
    turn = -pltpu.roll(w, LANES - 16, 1)
    for k in range(8):
        turn = turn + w[:, 16 + k : 17 + k] * coef[k : k + 1, :]
    turn = jnp.where((lane >= 8) & (lane < 16), turn, 0.0)
    weights = jnp.concatenate(
        [pltpu.roll(coef, LANES - 8, 1) + pltpu.roll(turn, 8, 1), -coef, -pltpu.roll(coef, 8, 1)], axis=0
    )[:, :24]
    f, a, n = (rows_of(parts, k, 3) for k in range(3))
    fields = jnp.concatenate([f, a, n], axis=0)
    new = lax.dot_general(weights, fields, (((0,), (0,)), ((), ())), precision=HIGHEST, preferred_element_type=jnp.float32)
    r = rows_of(rhs, 0, 1)
    for ref, v in ((sol, new[:8]), (resid, r + new[8:16]), (direction, f + new[16:24])):
        for t in range(16):
            ref[pl.ds(t, FIELDS, stride=16), :] = v[:, LANES * t : LANES * t + LANES]


def f32(*shape):
    return jax.ShapeDtypeStruct(shape, jnp.float32)


def local(rhs, classes, supports):
    sizes = {a: lax.axis_size(a) for a in ("z", "p", "h", "c", "x")}
    chips = sizes["z"] * sizes["p"] * 2
    upper_chip = lax.axis_index("h")
    pair = lax.axis_index("z") * sizes["p"] + lax.axis_index("p") + jnp.arange(-1, 2, dtype=jnp.int32)
    present = ((pair >= 0) & (pair < chips // 2)).astype(jnp.int32)
    core = lax.axis_index("c")
    where = jnp.concatenate([upper_chip[None].astype(jnp.int32), present, core[None].astype(jnp.int32)])
    chip = ("z", "p", "h")

    packed = pl.pallas_call(
        pack_kernel,
        out_shape=f32(16, 2, 2, 8, LANES),
        in_specs=[pl.BlockSpec(memory_space=pltpu.HBM)] * 3,
        out_specs=vmem(1)[0],
        scratch_shapes=[
            pltpu.VMEM((8, 2, 8, LANES), jnp.float32),
            pltpu.VMEM((2, 8, LANES), jnp.int32),
            pltpu.VMEM((2, 8, LANES), jnp.int32),
            pltpu.SemaphoreType.DMA((3,)),
        ],
        compiler_params=WIDE,
    )(rhs, classes, supports)
    own = lax.all_to_all(packed, ("x", "h", "c"), 0, 0)

    def moved(v, sources):
        return lax.ppermute(v, chip, [(s, i) for i, s in enumerate(sources) if 0 <= s < chips])

    far = moved(own, [i + 2 if i % 2 == 0 else i - 2 for i in range(chips)])
    swap = moved(own, [i - 1 if i % 2 == 0 else i + 1 for i in range(chips)])

    def partner(*blocks):
        n = len(blocks)
        grids = pl.pallas_call(
            grids_kernel,
            out_shape=f32(n, 16, 2, 8, LANES),
            in_specs=vmem(n),
            out_specs=vmem(1)[0],
            compiler_params=PARAMS,
        )(*blocks)
        return lax.ppermute(grids, "c", [(0, 1), (1, 0)])

    other = partner(own, swap, far)
    first, applied, *coefs = pl.pallas_call(
        first_kernel,
        out_shape=[f32(8, *TILE)] * 2 + [f32(24, *TILE)] * 3 + [f32(12, *TILE)],
        in_specs=smem() + vmem(4),
        out_specs=vmem(6),
        scratch_shapes=[pltpu.VMEM((10, *TILE), jnp.float32), pltpu.VMEM((24, *TILE), jnp.float32)] + work_shapes(),
        compiler_params=PARAMS,
    )(where, own, swap, far, other)
    below = moved(applied, [i - 2 for i in range(chips)])
    above = moved(applied, [i + 2 for i in range(chips)])
    results = pl.pallas_call(
        second_kernel,
        out_shape=f32(8, 3, 2, 8, LANES),
        in_specs=smem() + vmem(8),
        out_specs=vmem(1)[0],
        scratch_shapes=[pltpu.VMEM((24, *TILE), jnp.float32)] + work_shapes(),
        compiler_params=PARAMS,
    )(where, first, applied, below, above, *coefs)
    parts = lax.all_to_all(results, ("x", "c"), 0, 0).reshape(8 * 48, LANES)
    rows = rhs.reshape(8 * 16, LANES)

    tile = pl.pallas_call(
        gram_kernel, out_shape=f32(sizes["p"] * 4 * sizes["x"], 2, LANES), in_specs=vmem(2), out_specs=vmem(1)[0], compiler_params=PARAMS
    )(parts, rows)
    tile = lax.all_to_all(tile, ("x", "p", "h", "c"), 0, 0).sum(0)
    tile = jnp.broadcast_to(tile, (sizes["z"], 2, LANES))
    tile = lax.all_to_all(tile, "z", 0, 0)
    outs = pl.pallas_call(
        final_kernel,
        out_shape=[f32(128, LANES)] * 3,
        in_specs=vmem(3),
        out_specs=vmem(3),
        compiler_params=PARAMS,
    )(tile, parts, rows)
    return tuple(v.reshape(8, 2, 8, LANES) for v in outs)


def solution(mesh):
    gx, gy = mesh.shape["gx"], mesh.shape["gy"]
    y = min(8, gx // 2)
    fine = Mesh(mesh.devices.reshape(gx // (2 * y), y // 2, 2, 2, gy), ("z", "p", "h", "c", "x"))
    across = ("z", "p", "h", "c")
    grid = P(across, "x", None)
    fields = P(None, across, "x", None)
    return jax.shard_map(
        local, mesh=fine, in_specs=(fields, grid, grid), out_specs=(fields,) * 3, check_vma=False
    )
```

```python
import jax
import jax.numpy as jnp
from jax import lax
from jax.experimental import pallas as pl
from jax.experimental.pallas import tpu as pltpu
from jax.sharding import Mesh, PartitionSpec as P

SPRING = 8.0
OMEGA = 0.6
DAMP = 0.5
LANES = 128
FIELDS = 8
TILE = (4, 8, LANES)
HIGHEST = lax.Precision.HIGHEST
PARAMS = pltpu.CompilerParams(vmem_limit_bytes=24 * 1024 * 1024)
WIDE = pltpu.CompilerParams(vmem_limit_bytes=62 * 1024 * 1024)


def vmem(n):
    return [pl.BlockSpec(memory_space=pltpu.VMEM)] * n


def smem():
    return [pl.BlockSpec(memory_space=pltpu.SMEM)]


def iota(axis, shape=TILE):
    return lax.broadcasted_iota(jnp.int32, shape, axis)


def before_z(v):
    return jnp.where(iota(2) == 0, 0.0, pltpu.roll(v, 1, 2))


def after_z(v):
    return jnp.where(iota(2) == LANES - 1, 0.0, pltpu.roll(v, LANES - 1, 2))


def before_y(v):
    r = pltpu.roll(v, 1, 1)
    return jnp.where(iota(1) == 0, jnp.concatenate([jnp.zeros_like(r[:1]), r[:3]], axis=0), r)


def after_y(v):
    r = pltpu.roll(v, 7, 1)
    return jnp.where(iota(1) == 7, jnp.concatenate([r[1:], jnp.zeros_like(r[:1])], axis=0), r)


def pair_sum(v):
    v = (v + jnp.where(iota(1) % 2 == 0, pltpu.roll(v, 7, 1), pltpu.roll(v, 1, 1))).reshape(32, LANES)
    square = (LANES, LANES)
    ones = (iota(0, square) // 2 == iota(1, square) // 2).astype(jnp.bfloat16)
    high = v.astype(jnp.bfloat16)
    rest = v - high.astype(jnp.float32)
    middle = rest.astype(jnp.bfloat16)
    low = (rest - middle.astype(jnp.float32)).astype(jnp.bfloat16)
    pieces = jnp.concatenate([high, middle, low], axis=1)
    ones = jnp.concatenate([ones] * 3, axis=0)
    return jnp.dot(pieces, ones, preferred_element_type=jnp.float32).reshape(TILE)


def spread(u):
    low = before_z(u)
    out = []
    for f in (u + low, u - low):
        g = before_y(f)
        out += [f + g, f - g]
    return out


def element_plane(lower, upper, s16):
    s24, s48 = s16 * (2.0 / 3.0), s16 * (1.0 / 3.0)
    ss, ds, sd, dd = [(b + a, b - a) for a, b in zip(lower, upper)]
    w = ((s16 * ds[0], s24 * ds[1]), (s16 * sd[0], s24 * sd[1]), (s24 * dd[0], s48 * dd[1]))
    v = s16 * ss[1]
    return [-v] + [a - b for a, b in w], [v] + [a + b for a, b in w]


def gather(n):
    ss, ds, sd, dd = n
    ms = (ss + ds) + after_y(ss - ds)
    md = (sd + dd) + after_y(sd - dd)
    return (ms + md) + after_z(ms - md)


def apply_fine(u, s16, sp8, least, most):
    last, above = spread(u(least - 1)), None
    for e in range(least, most + 2):
        now = spread(u(e))
        to_lower, to_upper = element_plane(last, now, s16(e))
        if above is not None:
            yield e - 1, gather([a + b for a, b in zip(above, to_lower)]) + sp8(e - 1) * u(e - 1)
        last, above = now, to_upper


def restricted(even, odd, s16, least, most):
    last, above = (even if odd is None else odd)(least - 1), None
    for i in range(least, most + 2):
        now = even(i)
        to_lower, to_upper = element_plane(last, now, s16(2 * i))
        if above is not None:
            n = [a + b for a, b in zip(above, to_lower)]
            yield i - 1, gather([n[0]] + [a + b for a, b in zip(n[1:], inside)])
        if i <= most:
            last = now if odd is None else odd(i)
            inner = s16(2 * i + 1) * (4.0 if odd is None else 2.0)
            both = now if odd is None else [a + b for a, b in zip(now, last)]
            inside = [inner * both[1], inner * both[2], (inner * (2.0 / 3.0)) * both[3]]
        above = to_upper


def apply_coarse(c, s16, sp8, least, most):
    for i, h in restricted(lambda i: spread(c(i)), None, s16, least, most):
        yield i, pair_sum(h + (sp8(2 * i) + sp8(2 * i + 1)) * c(i))


def coarse_residual(source, u, s16, sp8, least, most):
    for i, h in restricted(lambda i: spread(u(2 * i)), lambda i: spread(u(2 * i + 1)), s16, least, most):
        a, b = 2 * i, 2 * i + 1
        yield i, pair_sum((source(a) - sp8(a) * u(a)) + (source(b) - sp8(b) * u(b)) - h)


class Planes:
    def __init__(self, ref, first, offset=None):
        self.ref, self.first, self.offset = ref, first, offset

    def at(self, p):
        return p - self.first if self.offset is None else p - self.first + self.offset

    def __call__(self, p):
        return self.ref[self.at(p)]

    def put(self, p, v):
        self.ref[self.at(p)] = v


def precondition(source, s16, sp8, dv, steps, work, least, most, emit):
    z, res, c, c1 = work
    lo, hi = (least - 1) // 2, (most + 1) // 2
    for p in range(2 * lo - 5, 2 * hi + 7):
        z.put(p, dv(p) * source(p))
    for i, r in coarse_residual(source, z, s16, sp8, lo - 2, hi + 2):
        res.put(i, r)
        c.put(i, steps(i) * r)
    for old, new, first, last in ((c, c1, lo - 1, hi + 1), (c1, c, lo, hi)):
        for i, a in apply_coarse(old, s16, sp8, first, last):
            new.put(i, old(i) + steps(i) * (res(i) - a))
    for p in range(least - 1, most + 2):
        z.put(p, z(p) + c(p // 2))
    for p, a in apply_fine(z, s16, sp8, least, most):
        emit(p, z(p) + dv(p) * (source(p) - a))


def work_shapes():
    plane = lambda n: pltpu.VMEM((n, *TILE), jnp.float32)
    return [plane(24), plane(12), plane(12), plane(12)]


def work_of(z, res, c, c1):
    return Planes(z, -8), Planes(res, -4), Planes(c, -4), Planes(c1, -4)


def pack_kernel(rhs, classes, supports, out, r, k, s, sems):
    copies = [pltpu.make_async_copy(a, b, sems.at[i]) for i, (a, b) in enumerate(((classes, k), (supports, s), (rhs, r)))]
    for copy in copies:
        copy.start()
    copies[0].wait()
    density = (k[...].astype(jnp.float32) + 1.0) / 4.0
    stiff = 0.001 + density * density * density
    for j in range(0, 16, 2):
        out[j, 0] = stiff
    copies[1].wait()
    support = s[...].astype(jnp.float32)
    for j in range(1, 16, 2):
        out[j, 0] = support
    copies[2].wait()
    for x in range(4):
        for c in range(2):
            v = r[x * 2 + c]
            for h in range(2):
                out[(x * 2 + h) * 2 + c, 1] = v


def grids_kernel(*refs):
    *blocks, out = refs
    for i, ref in enumerate(blocks):
        for j in range(16):
            out[i, j] = ref[j, 0]


def first_kernel(
    where, own, swap, far, other, first, applied, s16_out, sp8_out, dv_out, steps_out, out, source_ref, *work
):
    upper_chip, upper_core = where[0] != 0, where[4] != 0

    def block(ref, field, q):
        h, c = q // 4, (q // 2) % 2
        return jnp.stack([ref[(x * 2 + h) * 2 + c, *field, q % 2] for x in range(4)])

    def plane(field, p, grid=None):
        q = p % 8
        if 0 <= p < 8:
            return block(own if grid is None else grid.at[0], field, q)
        a, b = (swap, far) if grid is None else (grid.at[1], grid.at[2])
        a, b = block(a, field, q), block(b, field, q)
        return jnp.where(upper_chip, b, a) if p < 0 else jnp.where(upper_chip, a, b)

    def grids(p):
        a, b = plane((0,), p), plane((), p, other)
        return jnp.where(upper_core, b, a), jnp.where(upper_core, a, b)

    source, s16, sp8, dv = (Planes(r, -8) for r in (source_ref, s16_out, sp8_out, dv_out))
    steps, fields = Planes(steps_out, -4), Planes(out, -1)
    for p in range(-7, 15):
        source.put(p, plane((1,), p))
    sums = kept = None
    for p in range(-7, 16):
        t, support = grids(p)
        sp8.put(p, SPRING * support)
        s16.put(p, t * (1.0 / 16.0))
        t = t + after_z(t)
        t = t + after_y(t)
        if sums is not None:
            n = p - 1
            d = sp8(n) + (sums + t) * (1.0 / 3.0)
            ok = where[1 + (n + 8) // 8] != 0
            dv.put(n, jnp.where(ok, OMEGA / d, 0.0))
            if n % 2 and n > -7:
                steps.put(n // 2, jnp.where(ok, DAMP / pair_sum(kept + d), 0.0))
            kept = d
        sums = t

    def emit(p, v):
        fields.put(p, v)
        if 0 <= p < 8:
            first[p] = v

    precondition(source, s16, sp8, dv, steps, work_of(*work), -1, 8, emit)
    for p, v in apply_fine(fields, s16, sp8, 0, 7):
        applied[p] = v


def second_kernel(where, first, applied, below, above, s16_ref, sp8_ref, dv_ref, steps_ref, packed, source_ref, *work):
    shift = where[0] * 4
    for q in range(8):
        source_ref[q] = below[q]
        source_ref[8 + q] = applied[q]
        source_ref[16 + q] = above[q]
    source, s16, sp8, dv = (Planes(r, -8, shift) for r in (source_ref, s16_ref, sp8_ref, dv_ref))
    steps = Planes(steps_ref, -4, where[0] * 2)

    def put(field, p, v):
        for x in range(4):
            packed[x * 2 + p // 2, field, p % 2] = v[x]

    for p in range(4):
        put(0, p, first[shift + p])
        put(1, p, applied[shift + p])
    precondition(source, s16, sp8, dv, steps, work_of(*work), 0, 3, lambda p, v: put(2, p, v))


def rows_of(ref, field, fields):
    return jnp.concatenate(
        [ref[pl.ds(field * 16 + t, FIELDS, stride=fields * 16), :] for t in range(16)], axis=1
    )


def gram_kernel(parts, rhs, out):
    f, a, n = (rows_of(parts, k, 3) for k in range(3))
    r = rows_of(rhs, 0, 1)
    left = jnp.concatenate([f, a], axis=0)
    right = jnp.concatenate([a, r, n, f, jnp.zeros((LANES - 32, 2048), jnp.float32)], axis=0)
    g = lax.dot_general(left, right, (((1,), (1,)), ((), ())), precision=HIGHEST, preferred_element_type=jnp.float32)
    lane = iota(1, (8, LANES))
    tile = jnp.where(lane < 16, g[:8], jnp.where(lane < 32, g[8:], 0.0))
    turned = [tile] + [pltpu.roll(tile, 32 * m, 1) for m in range(1, 4)]
    short = jnp.concatenate([sum(turned[m][k + m : k + m + 1] for m in range(4)) for k in (0, 4)], axis=0)
    for k in range(out.shape[0]):
        out[k] = short


def final_kernel(sums, parts, rhs, sol, resid, direction):
    w = sums[0]
    for k in range(1, sums.shape[0]):
        w = w + sums[k]
    turned = [w] + [pltpu.roll(w, LANES - 32 * m, 1) for m in range(1, 4)]
    w = jnp.concatenate([turned[m][k : k + 1] for k in range(2) for m in range(4)], axis=0)
    shape = (8, LANES)
    lane, row = iota(1, shape), iota(0, shape)
    w = jnp.where(lane < 8, 0.5 * (w + pltpu.roll(w, LANES - 24, 1)), w)
    columns = [jnp.broadcast_to(w[:, k : k + 1], shape) for k in range(8)]
    scale = jnp.ones(shape, jnp.float32)
    for k in range(8):
        inverse = 1.0 / columns[k][k : k + 1, :]
        scale = jnp.where(row == k, inverse, scale)
        factor = jnp.where(row == k, 0.0, columns[k] * inverse)
        for j in range(k + 1, 8):
            columns[j] = columns[j] - factor * columns[j][k : k + 1, :]
        w = w - factor * w[k : k + 1, :]
    w = w * scale
    coef = jnp.where((lane >= 8) & (lane < 16), w, 0.0)
    turn = -pltpu.roll(w, LANES - 16, 1)
    for k in range(8):
        turn = turn + w[:, 16 + k : 17 + k] * coef[k : k + 1, :]
    turn = jnp.where((lane >= 8) & (lane < 16), turn, 0.0)
    weights = jnp.concatenate(
        [pltpu.roll(coef, LANES - 8, 1) + pltpu.roll(turn, 8, 1), -coef, -pltpu.roll(coef, 8, 1)], axis=0
    )[:, :24]
    f, a, n = (rows_of(parts, k, 3) for k in range(3))
    fields = jnp.concatenate([f, a, n], axis=0)
    new = lax.dot_general(weights, fields, (((0,), (0,)), ((), ())), precision=HIGHEST, preferred_element_type=jnp.float32)
    r = rows_of(rhs, 0, 1)
    for ref, v in ((sol, new[:8]), (resid, r + new[8:16]), (direction, f + new[16:24])):
        for t in range(16):
            ref[pl.ds(t, FIELDS, stride=16), :] = v[:, LANES * t : LANES * t + LANES]


def f32(*shape):
    return jax.ShapeDtypeStruct(shape, jnp.float32)


def local(rhs, classes, supports):
    sizes = {a: lax.axis_size(a) for a in ("z", "p", "h", "c", "x")}
    chips = sizes["z"] * sizes["p"] * 2
    upper_chip = lax.axis_index("h")
    pair = lax.axis_index("z") * sizes["p"] + lax.axis_index("p") + jnp.arange(-1, 2, dtype=jnp.int32)
    present = ((pair >= 0) & (pair < chips // 2)).astype(jnp.int32)
    core = lax.axis_index("c")
    where = jnp.concatenate([upper_chip[None].astype(jnp.int32), present, core[None].astype(jnp.int32)])
    chip = ("z", "p", "h")

    packed = pl.pallas_call(
        pack_kernel,
        out_shape=f32(16, 2, 2, 8, LANES),
        in_specs=[pl.BlockSpec(memory_space=pltpu.HBM)] * 3,
        out_specs=vmem(1)[0],
        scratch_shapes=[
            pltpu.VMEM((8, 2, 8, LANES), jnp.float32),
            pltpu.VMEM((2, 8, LANES), jnp.int32),
            pltpu.VMEM((2, 8, LANES), jnp.int32),
            pltpu.SemaphoreType.DMA((3,)),
        ],
        compiler_params=WIDE,
    )(rhs, classes, supports)
    own = lax.all_to_all(packed, ("x", "h", "c"), 0, 0)

    def moved(v, sources):
        return lax.ppermute(v, chip, [(s, i) for i, s in enumerate(sources) if 0 <= s < chips])

    far = moved(own, [i + 2 if i % 2 == 0 else i - 2 for i in range(chips)])
    swap = moved(own, [i - 1 if i % 2 == 0 else i + 1 for i in range(chips)])

    def partner(*blocks):
        n = len(blocks)
        grids = pl.pallas_call(
            grids_kernel,
            out_shape=f32(n, 16, 2, 8, LANES),
            in_specs=vmem(n),
            out_specs=vmem(1)[0],
            compiler_params=PARAMS,
        )(*blocks)
        return lax.ppermute(grids, "c", [(0, 1), (1, 0)])

    other = partner(own, swap, far)
    first, applied, *coefs = pl.pallas_call(
        first_kernel,
        out_shape=[f32(8, *TILE)] * 2 + [f32(24, *TILE)] * 3 + [f32(12, *TILE)],
        in_specs=smem() + vmem(4),
        out_specs=vmem(6),
        scratch_shapes=[pltpu.VMEM((10, *TILE), jnp.float32), pltpu.VMEM((24, *TILE), jnp.float32)] + work_shapes(),
        compiler_params=PARAMS,
    )(where, own, swap, far, other)
    below = moved(applied, [i - 2 for i in range(chips)])
    above = moved(applied, [i + 2 for i in range(chips)])
    results = pl.pallas_call(
        second_kernel,
        out_shape=f32(8, 3, 2, 8, LANES),
        in_specs=smem() + vmem(8),
        out_specs=vmem(1)[0],
        scratch_shapes=[pltpu.VMEM((24, *TILE), jnp.float32)] + work_shapes(),
        compiler_params=PARAMS,
    )(where, first, applied, below, above, *coefs)
    parts = lax.all_to_all(results, ("x", "c"), 0, 0).reshape(8 * 48, LANES)
    rows = rhs.reshape(8 * 16, LANES)

    tile = pl.pallas_call(
        gram_kernel, out_shape=f32(sizes["p"] * 4 * sizes["x"], 2, LANES), in_specs=vmem(2), out_specs=vmem(1)[0], compiler_params=PARAMS
    )(parts, rows)
    tile = lax.all_to_all(tile, ("x", "p", "h", "c"), 0, 0).sum(0)
    tile = jnp.broadcast_to(tile, (sizes["z"], 2, LANES))
    tile = lax.all_to_all(tile, "z", 0, 0)
    outs = pl.pallas_call(
        final_kernel,
        out_shape=[f32(128, LANES)] * 3,
        in_specs=vmem(3),
        out_specs=vmem(3),
        compiler_params=PARAMS,
    )(tile, parts, rows)
    return tuple(v.reshape(8, 2, 8, LANES) for v in outs)


def solution(mesh):
    gx, gy = mesh.shape["gx"], mesh.shape["gy"]
    y = min(8, gx // 2)
    fine = Mesh(mesh.devices.reshape(gx // (2 * y), y // 2, 2, 2, gy), ("z", "p", "h", "c", "x"))
    across = ("z", "p", "h", "c")
    grid = P(across, "x", None)
    fields = P(None, across, "x", None)
    return jax.shard_map(
        local, mesh=fine, in_specs=(fields, grid, grid), out_specs=(fields,) * 3, check_vma=False
    )
```

```python
import jax
import jax.numpy as jnp
from jax import lax
from jax.experimental import pallas as pl
from jax.experimental.pallas import tpu as pltpu
from jax.sharding import Mesh, PartitionSpec as P

SPRING = 8.0
OMEGA = 0.6
DAMP = 0.5
LANES = 128
FIELDS = 8
TILE = (4, 8, LANES)
HIGHEST = lax.Precision.HIGHEST
PARAMS = pltpu.CompilerParams(vmem_limit_bytes=24 * 1024 * 1024)
WIDE = pltpu.CompilerParams(vmem_limit_bytes=62 * 1024 * 1024)


def vmem(n):
    return [pl.BlockSpec(memory_space=pltpu.VMEM)] * n


def smem():
    return [pl.BlockSpec(memory_space=pltpu.SMEM)]


def iota(axis, shape=TILE):
    return lax.broadcasted_iota(jnp.int32, shape, axis)


def before_z(v):
    return jnp.where(iota(2) == 0, 0.0, pltpu.roll(v, 1, 2))


def after_z(v):
    return jnp.where(iota(2) == LANES - 1, 0.0, pltpu.roll(v, LANES - 1, 2))


def before_y(v):
    r = pltpu.roll(v, 1, 1)
    return jnp.where(iota(1) == 0, jnp.concatenate([jnp.zeros_like(r[:1]), r[:3]], axis=0), r)


def after_y(v):
    r = pltpu.roll(v, 7, 1)
    return jnp.where(iota(1) == 7, jnp.concatenate([r[1:], jnp.zeros_like(r[:1])], axis=0), r)


def pair_sum(v):
    v = (v + jnp.where(iota(1) % 2 == 0, pltpu.roll(v, 7, 1), pltpu.roll(v, 1, 1))).reshape(32, LANES)
    square = (LANES, LANES)
    ones = (iota(0, square) // 2 == iota(1, square) // 2).astype(jnp.bfloat16)
    high = v.astype(jnp.bfloat16)
    rest = v - high.astype(jnp.float32)
    middle = rest.astype(jnp.bfloat16)
    low = (rest - middle.astype(jnp.float32)).astype(jnp.bfloat16)
    pieces = jnp.concatenate([high, middle, low], axis=1)
    ones = jnp.concatenate([ones] * 3, axis=0)
    return jnp.dot(pieces, ones, preferred_element_type=jnp.float32).reshape(TILE)


def spread(u):
    low = before_z(u)
    out = []
    for f in (u + low, u - low):
        g = before_y(f)
        out += [f + g, f - g]
    return out


def element_plane(lower, upper, s16):
    s24, s48 = s16 * (2.0 / 3.0), s16 * (1.0 / 3.0)
    ss, ds, sd, dd = [(b + a, b - a) for a, b in zip(lower, upper)]
    w = ((s16 * ds[0], s24 * ds[1]), (s16 * sd[0], s24 * sd[1]), (s24 * dd[0], s48 * dd[1]))
    v = s16 * ss[1]
    return [-v] + [a - b for a, b in w], [v] + [a + b for a, b in w]


def gather(n):
    ss, ds, sd, dd = n
    ms = (ss + ds) + after_y(ss - ds)
    md = (sd + dd) + after_y(sd - dd)
    return (ms + md) + after_z(ms - md)


def apply_fine(u, s16, sp8, least, most):
    last, above = spread(u(least - 1)), None
    for e in range(least, most + 2):
        now = spread(u(e))
        to_lower, to_upper = element_plane(last, now, s16(e))
        if above is not None:
            yield e - 1, gather([a + b for a, b in zip(above, to_lower)]) + sp8(e - 1) * u(e - 1)
        last, above = now, to_upper


def restricted(even, odd, s16, least, most):
    last, above = (even if odd is None else odd)(least - 1), None
    for i in range(least, most + 2):
        now = even(i)
        to_lower, to_upper = element_plane(last, now, s16(2 * i))
        if above is not None:
            n = [a + b for a, b in zip(above, to_lower)]
            yield i - 1, gather([n[0]] + [a + b for a, b in zip(n[1:], inside)])
        if i <= most:
            last = now if odd is None else odd(i)
            inner = s16(2 * i + 1) * (4.0 if odd is None else 2.0)
            both = now if odd is None else [a + b for a, b in zip(now, last)]
            inside = [inner * both[1], inner * both[2], (inner * (2.0 / 3.0)) * both[3]]
        above = to_upper


def apply_coarse(c, s16, sp8, least, most):
    for i, h in restricted(lambda i: spread(c(i)), None, s16, least, most):
        yield i, pair_sum(h + (sp8(2 * i) + sp8(2 * i + 1)) * c(i))


def coarse_residual(source, u, s16, sp8, least, most):
    for i, h in restricted(lambda i: spread(u(2 * i)), lambda i: spread(u(2 * i + 1)), s16, least, most):
        a, b = 2 * i, 2 * i + 1
        yield i, pair_sum((source(a) - sp8(a) * u(a)) + (source(b) - sp8(b) * u(b)) - h)


class Planes:
    def __init__(self, ref, first, offset=None):
        self.ref, self.first, self.offset = ref, first, offset

    def at(self, p):
        return p - self.first if self.offset is None else p - self.first + self.offset

    def __call__(self, p):
        return self.ref[self.at(p)]

    def put(self, p, v):
        self.ref[self.at(p)] = v


def precondition(source, s16, sp8, dv, steps, work, least, most, emit):
    z, res, c, c1 = work
    lo, hi = (least - 1) // 2, (most + 1) // 2
    for p in range(2 * lo - 5, 2 * hi + 7):
        z.put(p, dv(p) * source(p))
    for i, r in coarse_residual(source, z, s16, sp8, lo - 2, hi + 2):
        res.put(i, r)
        c.put(i, steps(i) * r)
    for old, new, first, last in ((c, c1, lo - 1, hi + 1), (c1, c, lo, hi)):
        for i, a in apply_coarse(old, s16, sp8, first, last):
            new.put(i, old(i) + steps(i) * (res(i) - a))
    for p in range(least - 1, most + 2):
        z.put(p, z(p) + c(p // 2))
    for p, a in apply_fine(z, s16, sp8, least, most):
        emit(p, z(p) + dv(p) * (source(p) - a))


def work_shapes():
    plane = lambda n: pltpu.VMEM((n, *TILE), jnp.float32)
    return [plane(24), plane(12), plane(12), plane(12)]


def work_of(z, res, c, c1):
    return Planes(z, -8), Planes(res, -4), Planes(c, -4), Planes(c1, -4)


def pack_kernel(rhs, classes, supports, out, r, k, s, sems):
    copies = [pltpu.make_async_copy(a, b, sems.at[i]) for i, (a, b) in enumerate(((classes, k), (supports, s), (rhs, r)))]
    for copy in copies:
        copy.start()
    copies[0].wait()
    density = (k[...].astype(jnp.float32) + 1.0) / 4.0
    stiff = 0.001 + density * density * density
    for j in range(0, 16, 2):
        out[j, 0] = stiff
    copies[1].wait()
    support = s[...].astype(jnp.float32)
    for j in range(1, 16, 2):
        out[j, 0] = support
    copies[2].wait()
    for x in range(4):
        for c in range(2):
            v = r[x * 2 + c]
            for h in range(2):
                out[(x * 2 + h) * 2 + c, 1] = v


def grids_kernel(*refs):
    *blocks, out = refs
    for i, ref in enumerate(blocks):
        for j in range(16):
            out[i, j] = ref[j, 0]


def first_kernel(
    where, own, swap, far, grids, first, applied, s16_out, sp8_out, dv_out, steps_out, out, source_ref, *work
):
    upper_chip = where[0] != 0

    def plane(refs, p):
        q = p % 8
        h, c = q // 4, (q // 2) % 2
        block = lambda ref: jnp.stack([ref[(x * 2 + h) * 2 + c, q % 2] for x in range(4)])
        if 0 <= p < 8:
            return block(refs[0])
        a, b = block(refs[1]), block(refs[2])
        return jnp.where(upper_chip, b, a) if p < 0 else jnp.where(upper_chip, a, b)

    fields = [ref.at[:, 1] for ref in (own, swap, far)]
    stiffs, supports = ([grids.at[core, i] for i in range(3)] for core in range(2))
    source, s16, sp8, dv = (Planes(r, -8) for r in (source_ref, s16_out, sp8_out, dv_out))
    steps, new = Planes(steps_out, -4), Planes(out, -1)
    for p in range(-7, 15):
        source.put(p, plane(fields, p))
    sums = kept = None
    for p in range(-7, 16):
        t = plane(stiffs, p)
        sp8.put(p, SPRING * plane(supports, p))
        s16.put(p, t * (1.0 / 16.0))
        t = t + after_z(t)
        t = t + after_y(t)
        if sums is not None:
            n = p - 1
            d = sp8(n) + (sums + t) * (1.0 / 3.0)
            ok = where[1 + (n + 8) // 8] != 0
            dv.put(n, jnp.where(ok, OMEGA / d, 0.0))
            if n % 2 and n > -7:
                steps.put(n // 2, jnp.where(ok, DAMP / pair_sum(kept + d), 0.0))
            kept = d
        sums = t

    def emit(p, v):
        new.put(p, v)
        if 0 <= p < 8:
            first[p] = v

    precondition(source, s16, sp8, dv, steps, work_of(*work), -1, 8, emit)
    for p, v in apply_fine(new, s16, sp8, 0, 7):
        applied[p] = v


def second_kernel(where, first, applied, below, above, s16_ref, sp8_ref, dv_ref, steps_ref, packed, source_ref, *work):
    shift = where[0] * 4
    for q in range(8):
        source_ref[q] = below[q]
        source_ref[8 + q] = applied[q]
        source_ref[16 + q] = above[q]
    source, s16, sp8, dv = (Planes(r, -8, shift) for r in (source_ref, s16_ref, sp8_ref, dv_ref))
    steps = Planes(steps_ref, -4, where[0] * 2)

    def put(field, p, v):
        for x in range(4):
            packed[x * 2 + p // 2, field, p % 2] = v[x]

    for p in range(4):
        put(0, p, first[shift + p])
        put(1, p, applied[shift + p])
    precondition(source, s16, sp8, dv, steps, work_of(*work), 0, 3, lambda p, v: put(2, p, v))


def rows_of(ref, field, fields):
    return jnp.concatenate(
        [ref[pl.ds(field * 16 + t, FIELDS, stride=fields * 16), :] for t in range(16)], axis=1
    )


def gram_kernel(parts, rhs, out):
    f, a, n = (rows_of(parts, k, 3) for k in range(3))
    r = rows_of(rhs, 0, 1)
    left = jnp.concatenate([f, a], axis=0)
    right = jnp.concatenate([a, r, n, f, jnp.zeros((LANES - 32, 2048), jnp.float32)], axis=0)
    g = lax.dot_general(left, right, (((1,), (1,)), ((), ())), precision=HIGHEST, preferred_element_type=jnp.float32)
    lane = iota(1, (8, LANES))
    tile = jnp.where(lane < 16, g[:8], jnp.where(lane < 32, g[8:], 0.0))
    turned = [tile] + [pltpu.roll(tile, 32 * m, 1) for m in range(1, 4)]
    short = jnp.concatenate([sum(turned[m][k + m : k + m + 1] for m in range(4)) for k in (0, 4)], axis=0)
    for k in range(out.shape[0]):
        out[k] = short


def final_kernel(sums, parts, rhs, sol, resid, direction):
    w = sums[0]
    for k in range(1, sums.shape[0]):
        w = w + sums[k]
    turned = [w] + [pltpu.roll(w, LANES - 32 * m, 1) for m in range(1, 4)]
    w = jnp.concatenate([turned[m][k : k + 1] for k in range(2) for m in range(4)], axis=0)
    shape = (8, LANES)
    lane, row = iota(1, shape), iota(0, shape)
    w = jnp.where(lane < 8, 0.5 * (w + pltpu.roll(w, LANES - 24, 1)), w)
    columns = [jnp.broadcast_to(w[:, k : k + 1], shape) for k in range(8)]
    scale = jnp.ones(shape, jnp.float32)
    for k in range(8):
        inverse = 1.0 / columns[k][k : k + 1, :]
        scale = jnp.where(row == k, inverse, scale)
        factor = jnp.where(row == k, 0.0, columns[k] * inverse)
        for j in range(k + 1, 8):
            columns[j] = columns[j] - factor * columns[j][k : k + 1, :]
        w = w - factor * w[k : k + 1, :]
    w = w * scale
    coef = jnp.where((lane >= 8) & (lane < 16), w, 0.0)
    turn = -pltpu.roll(w, LANES - 16, 1)
    for k in range(8):
        turn = turn + w[:, 16 + k : 17 + k] * coef[k : k + 1, :]
    turn = jnp.where((lane >= 8) & (lane < 16), turn, 0.0)
    weights = jnp.concatenate(
        [pltpu.roll(coef, LANES - 8, 1) + pltpu.roll(turn, 8, 1), -coef, -pltpu.roll(coef, 8, 1)], axis=0
    )[:, :24]
    f, a, n = (rows_of(parts, k, 3) for k in range(3))
    fields = jnp.concatenate([f, a, n], axis=0)
    new = lax.dot_general(weights, fields, (((0,), (0,)), ((), ())), precision=HIGHEST, preferred_element_type=jnp.float32)
    r = rows_of(rhs, 0, 1)
    for ref, v in ((sol, new[:8]), (resid, r + new[8:16]), (direction, f + new[16:24])):
        for t in range(16):
            ref[pl.ds(t, FIELDS, stride=16), :] = v[:, LANES * t : LANES * t + LANES]


def f32(*shape):
    return jax.ShapeDtypeStruct(shape, jnp.float32)


def local(rhs, classes, supports):
    sizes = {a: lax.axis_size(a) for a in ("z", "p", "h", "c", "x")}
    chips = sizes["z"] * sizes["p"] * 2
    upper_chip = lax.axis_index("h")
    pair = lax.axis_index("z") * sizes["p"] + lax.axis_index("p") + jnp.arange(-1, 2, dtype=jnp.int32)
    present = ((pair >= 0) & (pair < chips // 2)).astype(jnp.int32)
    where = jnp.concatenate([upper_chip[None].astype(jnp.int32), present])
    chip = ("z", "p", "h")

    packed = pl.pallas_call(
        pack_kernel,
        out_shape=f32(16, 2, 2, 8, LANES),
        in_specs=[pl.BlockSpec(memory_space=pltpu.HBM)] * 3,
        out_specs=vmem(1)[0],
        scratch_shapes=[
            pltpu.VMEM((8, 2, 8, LANES), jnp.float32),
            pltpu.VMEM((2, 8, LANES), jnp.int32),
            pltpu.VMEM((2, 8, LANES), jnp.int32),
            pltpu.SemaphoreType.DMA((3,)),
        ],
        compiler_params=WIDE,
    )(rhs, classes, supports)
    own = lax.all_to_all(packed, ("x", "h", "c"), 0, 0)

    def moved(v, sources):
        return lax.ppermute(v, chip, [(s, i) for i, s in enumerate(sources) if 0 <= s < chips])

    far = moved(own, [i + 2 if i % 2 == 0 else i - 2 for i in range(chips)])
    swap = moved(own, [i - 1 if i % 2 == 0 else i + 1 for i in range(chips)])

    def both_cores(*blocks):
        n = len(blocks)
        grids = pl.pallas_call(
            grids_kernel,
            out_shape=f32(n, 16, 2, 8, LANES),
            in_specs=vmem(n),
            out_specs=vmem(1)[0],
            compiler_params=PARAMS,
        )(*blocks)
        return lax.all_gather(grids, "c")

    grids = both_cores(own, swap, far)
    first, applied, *coefs = pl.pallas_call(
        first_kernel,
        out_shape=[f32(8, *TILE)] * 2 + [f32(24, *TILE)] * 3 + [f32(12, *TILE)],
        in_specs=smem() + vmem(4),
        out_specs=vmem(6),
        scratch_shapes=[pltpu.VMEM((10, *TILE), jnp.float32), pltpu.VMEM((24, *TILE), jnp.float32)] + work_shapes(),
        compiler_params=PARAMS,
    )(where, own, swap, far, grids)
    below = moved(applied, [i - 2 for i in range(chips)])
    above = moved(applied, [i + 2 for i in range(chips)])
    results = pl.pallas_call(
        second_kernel,
        out_shape=f32(8, 3, 2, 8, LANES),
        in_specs=smem() + vmem(8),
        out_specs=vmem(1)[0],
        scratch_shapes=[pltpu.VMEM((24, *TILE), jnp.float32)] + work_shapes(),
        compiler_params=PARAMS,
    )(where, first, applied, below, above, *coefs)
    parts = lax.all_to_all(results, ("x", "c"), 0, 0).reshape(8 * 48, LANES)
    rows = rhs.reshape(8 * 16, LANES)

    tile = pl.pallas_call(
        gram_kernel, out_shape=f32(sizes["p"] * 4 * sizes["x"], 2, LANES), in_specs=vmem(2), out_specs=vmem(1)[0], compiler_params=PARAMS
    )(parts, rows)
    tile = lax.all_to_all(tile, ("x", "p", "h", "c"), 0, 0).sum(0)
    tile = jnp.broadcast_to(tile, (sizes["z"], 2, LANES))
    tile = lax.all_to_all(tile, "z", 0, 0)
    outs = pl.pallas_call(
        final_kernel,
        out_shape=[f32(128, LANES)] * 3,
        in_specs=vmem(3),
        out_specs=vmem(3),
        compiler_params=PARAMS,
    )(tile, parts, rows)
    return tuple(v.reshape(8, 2, 8, LANES) for v in outs)


def solution(mesh):
    gx, gy = mesh.shape["gx"], mesh.shape["gy"]
    y = min(8, gx // 2)
    fine = Mesh(mesh.devices.reshape(gx // (2 * y), y // 2, 2, 2, gy), ("z", "p", "h", "c", "x"))
    across = ("z", "p", "h", "c")
    grid = P(across, "x", None)
    fields = P(None, across, "x", None)
    return jax.shard_map(
        local, mesh=fine, in_specs=(fields, grid, grid), out_specs=(fields,) * 3, check_vma=False
    )
```

```python
import jax
import jax.numpy as jnp
from jax import lax
from jax.experimental import pallas as pl
from jax.experimental.pallas import tpu as pltpu
from jax.sharding import Mesh, PartitionSpec as P

SPRING = 8.0
OMEGA = 0.6
DAMP = 0.5
LANES = 128
FIELDS = 8
TILE = (4, 8, LANES)
HIGHEST = lax.Precision.HIGHEST
PARAMS = pltpu.CompilerParams(vmem_limit_bytes=24 * 1024 * 1024)
WIDE = pltpu.CompilerParams(vmem_limit_bytes=62 * 1024 * 1024)


def vmem(n):
    return [pl.BlockSpec(memory_space=pltpu.VMEM)] * n


def smem():
    return [pl.BlockSpec(memory_space=pltpu.SMEM)]


def iota(axis, shape=TILE):
    return lax.broadcasted_iota(jnp.int32, shape, axis)


def before_z(v):
    return jnp.where(iota(2) == 0, 0.0, pltpu.roll(v, 1, 2))


def after_z(v):
    return jnp.where(iota(2) == LANES - 1, 0.0, pltpu.roll(v, LANES - 1, 2))


def before_y(v):
    r = pltpu.roll(v, 1, 1)
    return jnp.where(iota(1) == 0, jnp.concatenate([jnp.zeros_like(r[:1]), r[:3]], axis=0), r)


def after_y(v):
    r = pltpu.roll(v, 7, 1)
    return jnp.where(iota(1) == 7, jnp.concatenate([r[1:], jnp.zeros_like(r[:1])], axis=0), r)


def pair_sum(v):
    v = (v + jnp.where(iota(1) % 2 == 0, pltpu.roll(v, 7, 1), pltpu.roll(v, 1, 1))).reshape(32, LANES)
    square = (LANES, LANES)
    ones = (iota(0, square) // 2 == iota(1, square) // 2).astype(jnp.bfloat16)
    high = v.astype(jnp.bfloat16)
    rest = v - high.astype(jnp.float32)
    middle = rest.astype(jnp.bfloat16)
    low = (rest - middle.astype(jnp.float32)).astype(jnp.bfloat16)
    pieces = jnp.concatenate([high, middle, low], axis=1)
    ones = jnp.concatenate([ones] * 3, axis=0)
    return jnp.dot(pieces, ones, preferred_element_type=jnp.float32).reshape(TILE)


def spread(u):
    low = before_z(u)
    out = []
    for f in (u + low, u - low):
        g = before_y(f)
        out += [f + g, f - g]
    return out


def element_plane(lower, upper, s16):
    s24, s48 = s16 * (2.0 / 3.0), s16 * (1.0 / 3.0)
    ss, ds, sd, dd = [(b + a, b - a) for a, b in zip(lower, upper)]
    w = ((s16 * ds[0], s24 * ds[1]), (s16 * sd[0], s24 * sd[1]), (s24 * dd[0], s48 * dd[1]))
    v = s16 * ss[1]
    return [-v] + [a - b for a, b in w], [v] + [a + b for a, b in w]


def gather(n):
    ss, ds, sd, dd = n
    ms = (ss + ds) + after_y(ss - ds)
    md = (sd + dd) + after_y(sd - dd)
    return (ms + md) + after_z(ms - md)


def apply_fine(u, s16, sp8, least, most):
    last, above = spread(u(least - 1)), None
    for e in range(least, most + 2):
        now = spread(u(e))
        to_lower, to_upper = element_plane(last, now, s16(e))
        if above is not None:
            yield e - 1, gather([a + b for a, b in zip(above, to_lower)]) + sp8(e - 1) * u(e - 1)
        last, above = now, to_upper


def restricted(even, odd, s16, least, most):
    last, above = (even if odd is None else odd)(least - 1), None
    for i in range(least, most + 2):
        now = even(i)
        to_lower, to_upper = element_plane(last, now, s16(2 * i))
        if above is not None:
            n = [a + b for a, b in zip(above, to_lower)]
            yield i - 1, gather([n[0]] + [a + b for a, b in zip(n[1:], inside)])
        if i <= most:
            last = now if odd is None else odd(i)
            inner = s16(2 * i + 1) * (4.0 if odd is None else 2.0)
            both = now if odd is None else [a + b for a, b in zip(now, last)]
            inside = [inner * both[1], inner * both[2], (inner * (2.0 / 3.0)) * both[3]]
        above = to_upper


def apply_coarse(c, s16, sp8, least, most):
    for i, h in restricted(lambda i: spread(c(i)), None, s16, least, most):
        yield i, pair_sum(h + (sp8(2 * i) + sp8(2 * i + 1)) * c(i))


def coarse_residual(source, u, s16, sp8, least, most):
    for i, h in restricted(lambda i: spread(u(2 * i)), lambda i: spread(u(2 * i + 1)), s16, least, most):
        a, b = 2 * i, 2 * i + 1
        yield i, pair_sum((source(a) - sp8(a) * u(a)) + (source(b) - sp8(b) * u(b)) - h)


class Planes:
    def __init__(self, ref, first, offset=None):
        self.ref, self.first, self.offset = ref, first, offset

    def at(self, p):
        return p - self.first if self.offset is None else p - self.first + self.offset

    def __call__(self, p):
        return self.ref[self.at(p)]

    def put(self, p, v):
        self.ref[self.at(p)] = v


def precondition(source, s16, sp8, dv, steps, work, least, most, emit):
    z, res, c, c1 = work
    lo, hi = (least - 1) // 2, (most + 1) // 2
    for p in range(2 * lo - 5, 2 * hi + 7):
        z.put(p, dv(p) * source(p))
    for i, r in coarse_residual(source, z, s16, sp8, lo - 2, hi + 2):
        res.put(i, r)
        c.put(i, steps(i) * r)
    for old, new, first, last in ((c, c1, lo - 1, hi + 1), (c1, c, lo, hi)):
        for i, a in apply_coarse(old, s16, sp8, first, last):
            new.put(i, old(i) + steps(i) * (res(i) - a))
    for p in range(least - 1, most + 2):
        z.put(p, z(p) + c(p // 2))
    for p, a in apply_fine(z, s16, sp8, least, most):
        emit(p, z(p) + dv(p) * (source(p) - a))


def work_shapes():
    plane = lambda n: pltpu.VMEM((n, *TILE), jnp.float32)
    return [plane(24), plane(12), plane(12), plane(12)]


def work_of(z, res, c, c1):
    return Planes(z, -8), Planes(res, -4), Planes(c, -4), Planes(c1, -4)


def pack_kernel(rhs, classes, supports, out, r, k, s, sems):
    copies = [pltpu.make_async_copy(a, b, sems.at[i]) for i, (a, b) in enumerate(((classes, k), (supports, s), (rhs, r)))]
    for copy in copies:
        copy.start()
    copies[0].wait()
    density = (k[...].astype(jnp.float32) + 1.0) / 4.0
    stiff = 0.001 + density * density * density
    for j in range(0, 16, 2):
        out[j, 0] = stiff
    copies[1].wait()
    support = s[...].astype(jnp.float32)
    for j in range(1, 16, 2):
        out[j, 0] = support
    copies[2].wait()
    for x in range(4):
        for c in range(2):
            v = r[x * 2 + c]
            for h in range(2):
                out[(x * 2 + h) * 2 + c, 1] = v


def grids_kernel(*refs):
    *blocks, out = refs
    for i, ref in enumerate(blocks):
        for j in range(16):
            out[i, j] = ref[j, 0]


def first_kernel(
    where, own, swap, far, grids, first, applied, s16_out, sp8_out, dv_out, steps_out, out, source_ref, *work
):
    upper_chip = where[0] != 0

    def plane(refs, p):
        q = p % 8
        h, c = q // 4, (q // 2) % 2
        block = lambda ref: jnp.stack([ref[(x * 2 + h) * 2 + c, q % 2] for x in range(4)])
        if 0 <= p < 8:
            return block(refs[0])
        a, b = block(refs[1]), block(refs[2])
        return jnp.where(upper_chip, b, a) if p < 0 else jnp.where(upper_chip, a, b)

    fields = [ref.at[:, 1] for ref in (own, swap, far)]
    stiffs, supports = ([grids.at[core, i] for i in range(3)] for core in range(2))
    source, s16, sp8, dv = (Planes(r, -8) for r in (source_ref, s16_out, sp8_out, dv_out))
    steps, new = Planes(steps_out, -4), Planes(out, -1)
    for p in range(-7, 15):
        source.put(p, plane(fields, p))
    sums = kept = None
    for p in range(-7, 16):
        t = plane(stiffs, p)
        sp8.put(p, SPRING * plane(supports, p))
        s16.put(p, t * (1.0 / 16.0))
        t = t + after_z(t)
        t = t + after_y(t)
        if sums is not None:
            n = p - 1
            d = sp8(n) + (sums + t) * (1.0 / 3.0)
            ok = where[1 + (n + 8) // 8] != 0
            dv.put(n, jnp.where(ok, OMEGA / d, 0.0))
            if n % 2 and n > -7:
                steps.put(n // 2, jnp.where(ok, DAMP / pair_sum(kept + d), 0.0))
            kept = d
        sums = t

    def emit(p, v):
        new.put(p, v)
        if 0 <= p < 8:
            first[p] = v

    precondition(source, s16, sp8, dv, steps, work_of(*work), -1, 8, emit)
    for p, v in apply_fine(new, s16, sp8, 0, 7):
        applied[p] = v


def second_kernel(where, first, applied, below, above, s16_ref, sp8_ref, dv_ref, steps_ref, packed, source_ref, *work):
    shift = where[0] * 4
    for q in range(8):
        source_ref[q] = below[q]
        source_ref[8 + q] = applied[q]
        source_ref[16 + q] = above[q]
    source, s16, sp8, dv = (Planes(r, -8, shift) for r in (source_ref, s16_ref, sp8_ref, dv_ref))
    steps = Planes(steps_ref, -4, where[0] * 2)

    def put(field, p, v):
        for x in range(4):
            packed[x * 2 + p // 2, field, p % 2] = v[x]

    for p in range(4):
        put(0, p, first[shift + p])
        put(1, p, applied[shift + p])
    precondition(source, s16, sp8, dv, steps, work_of(*work), 0, 3, lambda p, v: put(2, p, v))


def rows_of(ref, field, fields):
    return jnp.concatenate(
        [ref[pl.ds(field * 16 + t, FIELDS, stride=fields * 16), :] for t in range(16)], axis=1
    )


def gram_kernel(parts, rhs, out):
    f, a, n = (rows_of(parts, k, 3) for k in range(3))
    r = rows_of(rhs, 0, 1)
    left = jnp.concatenate([f, a], axis=0)
    right = jnp.concatenate([a, r, n, f, jnp.zeros((LANES - 32, 2048), jnp.float32)], axis=0)
    g = lax.dot_general(left, right, (((1,), (1,)), ((), ())), precision=HIGHEST, preferred_element_type=jnp.float32)
    lane = iota(1, (8, LANES))
    tile = jnp.where(lane < 16, g[:8], jnp.where(lane < 32, g[8:], 0.0))
    turned = [tile] + [pltpu.roll(tile, 32 * m, 1) for m in range(1, 4)]
    short = jnp.concatenate([sum(turned[m][k + m : k + m + 1] for m in range(4)) for k in (0, 4)], axis=0)
    for k in range(out.shape[0]):
        out[k] = short


def final_kernel(sums, parts, rhs, sol, resid, direction):
    w = sums[0]
    for k in range(1, sums.shape[0]):
        w = w + sums[k]
    turned = [w] + [pltpu.roll(w, LANES - 32 * m, 1) for m in range(1, 4)]
    w = jnp.concatenate([turned[m][k : k + 1] for k in range(2) for m in range(4)], axis=0)
    shape = (8, LANES)
    lane, row = iota(1, shape), iota(0, shape)
    w = jnp.where(lane < 8, 0.5 * (w + pltpu.roll(w, LANES - 24, 1)), w)
    columns = [jnp.broadcast_to(w[:, k : k + 1], shape) for k in range(8)]
    scale = jnp.ones(shape, jnp.float32)
    for k in range(8):
        inverse = 1.0 / columns[k][k : k + 1, :]
        scale = jnp.where(row == k, inverse, scale)
        factor = jnp.where(row == k, 0.0, columns[k] * inverse)
        for j in range(k + 1, 8):
            columns[j] = columns[j] - factor * columns[j][k : k + 1, :]
        w = w - factor * w[k : k + 1, :]
    w = w * scale
    coef = jnp.where((lane >= 8) & (lane < 16), w, 0.0)
    turn = -pltpu.roll(w, LANES - 16, 1)
    for k in range(8):
        turn = turn + w[:, 16 + k : 17 + k] * coef[k : k + 1, :]
    turn = jnp.where((lane >= 8) & (lane < 16), turn, 0.0)
    weights = jnp.concatenate(
        [pltpu.roll(coef, LANES - 8, 1) + pltpu.roll(turn, 8, 1), -coef, -pltpu.roll(coef, 8, 1)], axis=0
    )[:, :24]
    f, a, n = (rows_of(parts, k, 3) for k in range(3))
    fields = jnp.concatenate([f, a, n], axis=0)
    new = lax.dot_general(weights, fields, (((0,), (0,)), ((), ())), precision=HIGHEST, preferred_element_type=jnp.float32)
    r = rows_of(rhs, 0, 1)
    for ref, v in ((sol, new[:8]), (resid, r + new[8:16]), (direction, f + new[16:24])):
        for t in range(16):
            ref[pl.ds(t, FIELDS, stride=16), :] = v[:, LANES * t : LANES * t + LANES]


def f32(*shape):
    return jax.ShapeDtypeStruct(shape, jnp.float32)


def local(rhs, classes, supports):
    sizes = {a: lax.axis_size(a) for a in ("z", "p", "h", "c", "x")}
    chips = sizes["z"] * sizes["p"] * 2
    upper_chip = lax.axis_index("h")
    pair = lax.axis_index("z") * sizes["p"] + lax.axis_index("p") + jnp.arange(-1, 2, dtype=jnp.int32)
    present = ((pair >= 0) & (pair < chips // 2)).astype(jnp.int32)
    where = jnp.concatenate([upper_chip[None].astype(jnp.int32), present])
    chip = ("z", "p", "h")

    packed = pl.pallas_call(
        pack_kernel,
        out_shape=f32(16, 2, 2, 8, LANES),
        in_specs=[pl.BlockSpec(memory_space=pltpu.HBM)] * 3,
        out_specs=vmem(1)[0],
        scratch_shapes=[
            pltpu.VMEM((8, 2, 8, LANES), jnp.float32),
            pltpu.VMEM((2, 8, LANES), jnp.int32),
            pltpu.VMEM((2, 8, LANES), jnp.int32),
            pltpu.SemaphoreType.DMA((3,)),
        ],
        compiler_params=WIDE,
    )(rhs, classes, supports)
    own = lax.all_to_all(packed, ("x", "h", "c"), 0, 0)

    def moved(v, sources):
        return lax.ppermute(v, chip, [(s, i) for i, s in enumerate(sources) if 0 <= s < chips])

    far = moved(own, [i + 2 if i % 2 == 0 else i - 2 for i in range(chips)])
    swap = moved(own, [i - 1 if i % 2 == 0 else i + 1 for i in range(chips)])

    def both_cores(*blocks):
        n = len(blocks)
        grids = pl.pallas_call(
            grids_kernel,
            out_shape=f32(n, 16, 2, 8, LANES),
            in_specs=vmem(n),
            out_specs=vmem(1)[0],
            compiler_params=PARAMS,
        )(*blocks)
        return lax.all_gather(grids, "c")

    grids = both_cores(own, swap, far)
    first, applied, *coefs = pl.pallas_call(
        first_kernel,
        out_shape=[f32(8, *TILE)] * 2 + [f32(24, *TILE)] * 3 + [f32(12, *TILE)],
        in_specs=smem() + vmem(4),
        out_specs=vmem(6),
        scratch_shapes=[pltpu.VMEM((10, *TILE), jnp.float32), pltpu.VMEM((24, *TILE), jnp.float32)] + work_shapes(),
        compiler_params=PARAMS,
    )(where, own, swap, far, grids)
    below = moved(applied, [i - 2 for i in range(chips)])
    above = moved(applied, [i + 2 for i in range(chips)])
    results = pl.pallas_call(
        second_kernel,
        out_shape=f32(8, 3, 2, 8, LANES),
        in_specs=smem() + vmem(8),
        out_specs=vmem(1)[0],
        scratch_shapes=[pltpu.VMEM((24, *TILE), jnp.float32)] + work_shapes(),
        compiler_params=PARAMS,
    )(where, first, applied, below, above, *coefs)
    parts = lax.all_to_all(results, ("x", "c"), 0, 0).reshape(8 * 48, LANES)
    rows = rhs.reshape(8 * 16, LANES)

    tile = pl.pallas_call(
        gram_kernel, out_shape=f32(sizes["x"] * sizes["z"], 2, LANES), in_specs=vmem(2), out_specs=vmem(1)[0], compiler_params=PARAMS
    )(parts, rows)
    tile = lax.all_to_all(tile, ("x", "z"), 0, 0).sum(0)
    tile = jnp.broadcast_to(tile, (sizes["p"] * 4, 2, LANES))
    tile = lax.all_to_all(tile, ("p", "h", "c"), 0, 0)
    outs = pl.pallas_call(
        final_kernel,
        out_shape=[f32(128, LANES)] * 3,
        in_specs=vmem(3),
        out_specs=vmem(3),
        compiler_params=PARAMS,
    )(tile, parts, rows)
    return tuple(v.reshape(8, 2, 8, LANES) for v in outs)


def solution(mesh):
    gx, gy = mesh.shape["gx"], mesh.shape["gy"]
    y = min(8, gx // 2)
    fine = Mesh(mesh.devices.reshape(gx // (2 * y), y // 2, 2, 2, gy), ("z", "p", "h", "c", "x"))
    across = ("z", "p", "h", "c")
    grid = P(across, "x", None)
    fields = P(None, across, "x", None)
    return jax.shard_map(
        local, mesh=fine, in_specs=(fields, grid, grid), out_specs=(fields,) * 3, check_vma=False
    )
```

```python
import jax
import jax.numpy as jnp
from jax import lax
from jax.experimental import pallas as pl
from jax.experimental.pallas import tpu as pltpu
from jax.sharding import Mesh, PartitionSpec as P

SPRING = 8.0
OMEGA = 0.6
DAMP = 0.5
LANES = 128
FIELDS = 8
TILE = (4, 8, LANES)
HIGHEST = lax.Precision.HIGHEST
PARAMS = pltpu.CompilerParams(vmem_limit_bytes=24 * 1024 * 1024)
WIDE = pltpu.CompilerParams(vmem_limit_bytes=62 * 1024 * 1024)


def vmem(n):
    return [pl.BlockSpec(memory_space=pltpu.VMEM)] * n


def iota(axis, shape=TILE):
    return lax.broadcasted_iota(jnp.int32, shape, axis)


def before_z(v):
    return jnp.where(iota(2) == 0, 0.0, pltpu.roll(v, 1, 2))


def after_z(v):
    return jnp.where(iota(2) == LANES - 1, 0.0, pltpu.roll(v, LANES - 1, 2))


def before_y(v):
    r = pltpu.roll(v, 1, 1)
    return jnp.where(iota(1) == 0, jnp.concatenate([jnp.zeros_like(r[:1]), r[:3]], axis=0), r)


def after_y(v):
    r = pltpu.roll(v, 7, 1)
    return jnp.where(iota(1) == 7, jnp.concatenate([r[1:], jnp.zeros_like(r[:1])], axis=0), r)


def pair_sum(v):
    v = (v + jnp.where(iota(1) % 2 == 0, pltpu.roll(v, 7, 1), pltpu.roll(v, 1, 1))).reshape(32, LANES)
    square = (LANES, LANES)
    ones = (iota(0, square) // 2 == iota(1, square) // 2).astype(jnp.bfloat16)
    high = v.astype(jnp.bfloat16)
    rest = v - high.astype(jnp.float32)
    middle = rest.astype(jnp.bfloat16)
    low = (rest - middle.astype(jnp.float32)).astype(jnp.bfloat16)
    pieces = jnp.concatenate([high, middle, low], axis=1)
    ones = jnp.concatenate([ones] * 3, axis=0)
    return jnp.dot(pieces, ones, preferred_element_type=jnp.float32).reshape(TILE)


def spread(u):
    low = before_z(u)
    out = []
    for f in (u + low, u - low):
        g = before_y(f)
        out += [f + g, f - g]
    return out


def element_plane(lower, upper, s16):
    s24, s48 = s16 * (2.0 / 3.0), s16 * (1.0 / 3.0)
    ss, ds, sd, dd = [(b + a, b - a) for a, b in zip(lower, upper)]
    w = ((s16 * ds[0], s24 * ds[1]), (s16 * sd[0], s24 * sd[1]), (s24 * dd[0], s48 * dd[1]))
    v = s16 * ss[1]
    return [-v] + [a - b for a, b in w], [v] + [a + b for a, b in w]


def gather(n):
    ss, ds, sd, dd = n
    ms = (ss + ds) + after_y(ss - ds)
    md = (sd + dd) + after_y(sd - dd)
    return (ms + md) + after_z(ms - md)


def apply_fine(u, s16, sp8, least, most):
    last, above = spread(u(least - 1)), None
    for e in range(least, most + 2):
        now = spread(u(e))
        to_lower, to_upper = element_plane(last, now, s16(e))
        if above is not None:
            yield e - 1, gather([a + b for a, b in zip(above, to_lower)]) + sp8(e - 1) * u(e - 1)
        last, above = now, to_upper


def restricted(even, odd, s16, least, most):
    last, above = (even if odd is None else odd)(least - 1), None
    for i in range(least, most + 2):
        now = even(i)
        to_lower, to_upper = element_plane(last, now, s16(2 * i))
        if above is not None:
            n = [a + b for a, b in zip(above, to_lower)]
            yield i - 1, gather([n[0]] + [a + b for a, b in zip(n[1:], inside)])
        if i <= most:
            last = now if odd is None else odd(i)
            inner = s16(2 * i + 1) * (4.0 if odd is None else 2.0)
            both = now if odd is None else [a + b for a, b in zip(now, last)]
            inside = [inner * both[1], inner * both[2], (inner * (2.0 / 3.0)) * both[3]]
        above = to_upper


def apply_coarse(c, s16, sp8, least, most):
    for i, h in restricted(lambda i: spread(c(i)), None, s16, least, most):
        yield i, pair_sum(h + (sp8(2 * i) + sp8(2 * i + 1)) * c(i))


def coarse_residual(source, u, s16, sp8, least, most):
    for i, h in restricted(lambda i: spread(u(2 * i)), lambda i: spread(u(2 * i + 1)), s16, least, most):
        a, b = 2 * i, 2 * i + 1
        yield i, pair_sum((source(a) - sp8(a) * u(a)) + (source(b) - sp8(b) * u(b)) - h)


class Planes:
    def __init__(self, ref, first, offset=None):
        self.ref, self.first, self.offset = ref, first, offset

    def at(self, p):
        return p - self.first if self.offset is None else p - self.first + self.offset

    def __call__(self, p):
        return self.ref[self.at(p)]

    def put(self, p, v):
        self.ref[self.at(p)] = v


def precondition(source, s16, sp8, dv, steps, work, least, most, emit):
    z, res, c, c1 = work
    lo, hi = (least - 1) // 2, (most + 1) // 2
    for p in range(2 * lo - 5, 2 * hi + 7):
        z.put(p, dv(p) * source(p))
    for i, r in coarse_residual(source, z, s16, sp8, lo - 2, hi + 2):
        res.put(i, r)
        c.put(i, steps(i) * r)
    for old, new, first, last in ((c, c1, lo - 1, hi + 1), (c1, c, lo, hi)):
        for i, a in apply_coarse(old, s16, sp8, first, last):
            new.put(i, old(i) + steps(i) * (res(i) - a))
    for p in range(least - 1, most + 2):
        z.put(p, z(p) + c(p // 2))
    for p, a in apply_fine(z, s16, sp8, least, most):
        emit(p, z(p) + dv(p) * (source(p) - a))


def work_shapes():
    plane = lambda n: pltpu.VMEM((n, *TILE), jnp.float32)
    return [plane(24), plane(12), plane(12), plane(12)]


def work_of(z, res, c, c1):
    return Planes(z, -8), Planes(res, -4), Planes(c, -4), Planes(c1, -4)


def pack_kernel(rhs, classes, supports, out, r, k, s, sems):
    copies = [pltpu.make_async_copy(a, b, sems.at[i]) for i, (a, b) in enumerate(((classes, k), (supports, s), (rhs, r)))]
    for copy in copies:
        copy.start()
    copies[0].wait()
    density = (k[...].astype(jnp.float32) + 1.0) / 4.0
    stiff = 0.001 + density * density * density
    for j in range(0, 16, 2):
        out[j, 0] = stiff
    copies[1].wait()
    support = s[...].astype(jnp.float32)
    for j in range(1, 16, 2):
        out[j, 0] = support
    copies[2].wait()
    for x in range(4):
        for c in range(2):
            v = r[x * 2 + c]
            for h in range(2):
                out[(x * 2 + h) * 2 + c, 1] = v


def my_place():
    pair = lax.axis_index("z") * lax.axis_size("p") + lax.axis_index("p")
    return lax.axis_index("h"), pair, lax.axis_size("z") * lax.axis_size("p")


def grids_kernel(*refs):
    *blocks, out = refs
    for i, ref in enumerate(blocks):
        for j in range(16):
            out[i, j] = ref[j, 0]


def first_kernel(
    own, swap, far, grids, first, applied, s16_out, sp8_out, dv_out, steps_out, out, source_ref, *work
):
    h, pair, pairs = my_place()
    upper_chip = h != 0
    present = (pair > 0, pair >= 0, pair < pairs - 1)

    def plane(refs, p):
        q = p % 8
        h, c = q // 4, (q // 2) % 2
        block = lambda ref: jnp.stack([ref[(x * 2 + h) * 2 + c, q % 2] for x in range(4)])
        if 0 <= p < 8:
            return block(refs[0])
        a, b = block(refs[1]), block(refs[2])
        return jnp.where(upper_chip, b, a) if p < 0 else jnp.where(upper_chip, a, b)

    fields = [ref.at[:, 1] for ref in (own, swap, far)]
    stiffs, supports = ([grids.at[core, i] for i in range(3)] for core in range(2))
    source, s16, sp8, dv = (Planes(r, -8) for r in (source_ref, s16_out, sp8_out, dv_out))
    steps, new = Planes(steps_out, -4), Planes(out, -1)
    for p in range(-7, 15):
        source.put(p, plane(fields, p))
    sums = kept = None
    for p in range(-7, 16):
        t = plane(stiffs, p)
        sp8.put(p, SPRING * plane(supports, p))
        s16.put(p, t * (1.0 / 16.0))
        t = t + after_z(t)
        t = t + after_y(t)
        if sums is not None:
            n = p - 1
            d = sp8(n) + (sums + t) * (1.0 / 3.0)
            ok = present[(n + 8) // 8]
            dv.put(n, jnp.where(ok, OMEGA / d, 0.0))
            if n % 2 and n > -7:
                steps.put(n // 2, jnp.where(ok, DAMP / pair_sum(kept + d), 0.0))
            kept = d
        sums = t

    def emit(p, v):
        new.put(p, v)
        if 0 <= p < 8:
            first[p] = v

    precondition(source, s16, sp8, dv, steps, work_of(*work), -1, 8, emit)
    for p, v in apply_fine(new, s16, sp8, 0, 7):
        applied[p] = v


def second_kernel(first, applied, below, above, s16_ref, sp8_ref, dv_ref, steps_ref, packed, source_ref, *work):
    h, _, _ = my_place()
    shift = h * 4
    for q in range(8):
        source_ref[q] = below[q]
        source_ref[8 + q] = applied[q]
        source_ref[16 + q] = above[q]
    source, s16, sp8, dv = (Planes(r, -8, shift) for r in (source_ref, s16_ref, sp8_ref, dv_ref))
    steps = Planes(steps_ref, -4, h * 2)

    def put(field, p, v):
        for x in range(4):
            packed[x * 2 + p // 2, field, p % 2] = v[x]

    for p in range(4):
        put(0, p, first[shift + p])
        put(1, p, applied[shift + p])
    precondition(source, s16, sp8, dv, steps, work_of(*work), 0, 3, lambda p, v: put(2, p, v))


def rows_of(ref, field, fields):
    return jnp.concatenate(
        [ref[pl.ds(field * 16 + t, FIELDS, stride=fields * 16), :] for t in range(16)], axis=1
    )


def gram_kernel(parts, rhs, out):
    f, a, n = (rows_of(parts, k, 3) for k in range(3))
    r = rows_of(rhs, 0, 1)
    left = jnp.concatenate([f, a], axis=0)
    right = jnp.concatenate([a, r, n, f, jnp.zeros((LANES - 32, 2048), jnp.float32)], axis=0)
    g = lax.dot_general(left, right, (((1,), (1,)), ((), ())), precision=HIGHEST, preferred_element_type=jnp.float32)
    lane = iota(1, (8, LANES))
    tile = jnp.where(lane < 16, g[:8], jnp.where(lane < 32, g[8:], 0.0))
    turned = [tile] + [pltpu.roll(tile, 32 * m, 1) for m in range(1, 4)]
    short = jnp.concatenate([sum(turned[m][k + m : k + m + 1] for m in range(4)) for k in (0, 4)], axis=0)
    for k in range(out.shape[0]):
        out[k] = short


def final_kernel(sums, parts, rhs, sol, resid, direction):
    w = sums[0]
    for k in range(1, sums.shape[0]):
        w = w + sums[k]
    turned = [w] + [pltpu.roll(w, LANES - 32 * m, 1) for m in range(1, 4)]
    w = jnp.concatenate([turned[m][k : k + 1] for k in range(2) for m in range(4)], axis=0)
    shape = (8, LANES)
    lane, row = iota(1, shape), iota(0, shape)
    w = jnp.where(lane < 8, 0.5 * (w + pltpu.roll(w, LANES - 24, 1)), w)
    columns = [jnp.broadcast_to(w[:, k : k + 1], shape) for k in range(8)]
    scale = jnp.ones(shape, jnp.float32)
    for k in range(8):
        inverse = 1.0 / columns[k][k : k + 1, :]
        scale = jnp.where(row == k, inverse, scale)
        factor = jnp.where(row == k, 0.0, columns[k] * inverse)
        for j in range(k + 1, 8):
            columns[j] = columns[j] - factor * columns[j][k : k + 1, :]
        w = w - factor * w[k : k + 1, :]
    w = w * scale
    coef = jnp.where((lane >= 8) & (lane < 16), w, 0.0)
    turn = -pltpu.roll(w, LANES - 16, 1)
    for k in range(8):
        turn = turn + w[:, 16 + k : 17 + k] * coef[k : k + 1, :]
    turn = jnp.where((lane >= 8) & (lane < 16), turn, 0.0)
    weights = jnp.concatenate(
        [pltpu.roll(coef, LANES - 8, 1) + pltpu.roll(turn, 8, 1), -coef, -pltpu.roll(coef, 8, 1)], axis=0
    )[:, :24]
    f, a, n = (rows_of(parts, k, 3) for k in range(3))
    fields = jnp.concatenate([f, a, n], axis=0)
    new = lax.dot_general(weights, fields, (((0,), (0,)), ((), ())), precision=HIGHEST, preferred_element_type=jnp.float32)
    r = rows_of(rhs, 0, 1)
    for ref, v in ((sol, new[:8]), (resid, r + new[8:16]), (direction, f + new[16:24])):
        for t in range(16):
            ref[pl.ds(t, FIELDS, stride=16), :] = v[:, LANES * t : LANES * t + LANES]


def f32(*shape):
    return jax.ShapeDtypeStruct(shape, jnp.float32)


def local(rhs, classes, supports):
    sizes = {a: lax.axis_size(a) for a in ("z", "p", "h", "c", "x")}
    chips = sizes["z"] * sizes["p"] * 2
    chip = ("z", "p", "h")

    packed = pl.pallas_call(
        pack_kernel,
        out_shape=f32(16, 2, 2, 8, LANES),
        in_specs=[pl.BlockSpec(memory_space=pltpu.HBM)] * 3,
        out_specs=vmem(1)[0],
        scratch_shapes=[
            pltpu.VMEM((8, 2, 8, LANES), jnp.float32),
            pltpu.VMEM((2, 8, LANES), jnp.int32),
            pltpu.VMEM((2, 8, LANES), jnp.int32),
            pltpu.SemaphoreType.DMA((3,)),
        ],
        compiler_params=WIDE,
    )(rhs, classes, supports)
    own = lax.all_to_all(packed, ("x", "h", "c"), 0, 0)

    def moved(v, sources):
        return lax.ppermute(v, chip, [(s, i) for i, s in enumerate(sources) if 0 <= s < chips])

    far = moved(own, [i + 2 if i % 2 == 0 else i - 2 for i in range(chips)])
    swap = moved(own, [i - 1 if i % 2 == 0 else i + 1 for i in range(chips)])

    def both_cores(*blocks):
        n = len(blocks)
        grids = pl.pallas_call(
            grids_kernel,
            out_shape=f32(n, 16, 2, 8, LANES),
            in_specs=vmem(n),
            out_specs=vmem(1)[0],
            compiler_params=PARAMS,
        )(*blocks)
        return lax.all_gather(grids, "c")

    grids = both_cores(own, swap, far)
    first, applied, *coefs = pl.pallas_call(
        first_kernel,
        out_shape=[f32(8, *TILE)] * 2 + [f32(24, *TILE)] * 3 + [f32(12, *TILE)],
        in_specs=vmem(4),
        out_specs=vmem(6),
        scratch_shapes=[pltpu.VMEM((10, *TILE), jnp.float32), pltpu.VMEM((24, *TILE), jnp.float32)] + work_shapes(),
        compiler_params=PARAMS,
    )(own, swap, far, grids)
    below = moved(applied, [i - 2 for i in range(chips)])
    above = moved(applied, [i + 2 for i in range(chips)])
    results = pl.pallas_call(
        second_kernel,
        out_shape=f32(8, 3, 2, 8, LANES),
        in_specs=vmem(8),
        out_specs=vmem(1)[0],
        scratch_shapes=[pltpu.VMEM((24, *TILE), jnp.float32)] + work_shapes(),
        compiler_params=PARAMS,
    )(first, applied, below, above, *coefs)
    parts = lax.all_to_all(results, ("x", "c"), 0, 0).reshape(8 * 48, LANES)
    rows = rhs.reshape(8 * 16, LANES)

    tile = pl.pallas_call(
        gram_kernel, out_shape=f32(sizes["p"] * 4 * sizes["x"], 2, LANES), in_specs=vmem(2), out_specs=vmem(1)[0], compiler_params=PARAMS
    )(parts, rows)
    tile = lax.all_to_all(tile, ("x", "p", "h", "c"), 0, 0).sum(0)
    tile = jnp.broadcast_to(tile, (sizes["z"], 2, LANES))
    tile = lax.all_to_all(tile, "z", 0, 0)
    outs = pl.pallas_call(
        final_kernel,
        out_shape=[f32(128, LANES)] * 3,
        in_specs=vmem(3),
        out_specs=vmem(3),
        compiler_params=PARAMS,
    )(tile, parts, rows)
    return tuple(v.reshape(8, 2, 8, LANES) for v in outs)


def solution(mesh):
    gx, gy = mesh.shape["gx"], mesh.shape["gy"]
    y = min(8, gx // 2)
    fine = Mesh(mesh.devices.reshape(gx // (2 * y), y // 2, 2, 2, gy), ("z", "p", "h", "c", "x"))
    across = ("z", "p", "h", "c")
    grid = P(across, "x", None)
    fields = P(None, across, "x", None)
    return jax.shard_map(
        local, mesh=fine, in_specs=(fields, grid, grid), out_specs=(fields,) * 3, check_vma=False
    )
```

```python
import jax
import jax.numpy as jnp
from jax import lax
from jax.experimental import pallas as pl
from jax.experimental.pallas import tpu as pltpu
from jax.sharding import Mesh, PartitionSpec as P

SPRING = 8.0
OMEGA = 0.6
DAMP = 0.5
LANES = 128
FIELDS = 8
TILE = (4, 8, LANES)
HIGHEST = lax.Precision.HIGHEST
PARAMS = pltpu.CompilerParams(vmem_limit_bytes=24 * 1024 * 1024)
WIDE = pltpu.CompilerParams(vmem_limit_bytes=62 * 1024 * 1024)


def vmem(n):
    return [pl.BlockSpec(memory_space=pltpu.VMEM)] * n


def iota(axis, shape=TILE):
    return lax.broadcasted_iota(jnp.int32, shape, axis)


def before_z(v):
    return jnp.where(iota(2) == 0, 0.0, pltpu.roll(v, 1, 2))


def after_z(v):
    return jnp.where(iota(2) == LANES - 1, 0.0, pltpu.roll(v, LANES - 1, 2))


def before_y(v):
    r = pltpu.roll(v, 1, 1)
    return jnp.where(iota(1) == 0, jnp.concatenate([jnp.zeros_like(r[:1]), r[:3]], axis=0), r)


def after_y(v):
    r = pltpu.roll(v, 7, 1)
    return jnp.where(iota(1) == 7, jnp.concatenate([r[1:], jnp.zeros_like(r[:1])], axis=0), r)


def pair_sum(v):
    v = (v + jnp.where(iota(1) % 2 == 0, pltpu.roll(v, 7, 1), pltpu.roll(v, 1, 1))).reshape(32, LANES)
    square = (LANES, LANES)
    ones = (iota(0, square) // 2 == iota(1, square) // 2).astype(jnp.bfloat16)
    high = v.astype(jnp.bfloat16)
    rest = v - high.astype(jnp.float32)
    middle = rest.astype(jnp.bfloat16)
    low = (rest - middle.astype(jnp.float32)).astype(jnp.bfloat16)
    pieces = jnp.concatenate([high, middle, low], axis=1)
    ones = jnp.concatenate([ones] * 3, axis=0)
    return jnp.dot(pieces, ones, preferred_element_type=jnp.float32).reshape(TILE)


def spread(u):
    low = before_z(u)
    out = []
    for f in (u + low, u - low):
        g = before_y(f)
        out += [f + g, f - g]
    return out


def element_plane(lower, upper, s16):
    s24, s48 = s16 * (2.0 / 3.0), s16 * (1.0 / 3.0)
    ss, ds, sd, dd = [(b + a, b - a) for a, b in zip(lower, upper)]
    w = ((s16 * ds[0], s24 * ds[1]), (s16 * sd[0], s24 * sd[1]), (s24 * dd[0], s48 * dd[1]))
    v = s16 * ss[1]
    return [-v] + [a - b for a, b in w], [v] + [a + b for a, b in w]


def gather(n):
    ss, ds, sd, dd = n
    ms = (ss + ds) + after_y(ss - ds)
    md = (sd + dd) + after_y(sd - dd)
    return (ms + md) + after_z(ms - md)


def apply_fine(u, s16, sp8, least, most):
    last, above = spread(u(least - 1)), None
    for e in range(least, most + 2):
        now = spread(u(e))
        to_lower, to_upper = element_plane(last, now, s16(e))
        if above is not None:
            yield e - 1, gather([a + b for a, b in zip(above, to_lower)]) + sp8(e - 1) * u(e - 1)
        last, above = now, to_upper


def restricted(even, odd, s16, least, most):
    last, above = (even if odd is None else odd)(least - 1), None
    for i in range(least, most + 2):
        now = even(i)
        to_lower, to_upper = element_plane(last, now, s16(2 * i))
        if above is not None:
            n = [a + b for a, b in zip(above, to_lower)]
            yield i - 1, gather([n[0]] + [a + b for a, b in zip(n[1:], inside)])
        if i <= most:
            last = now if odd is None else odd(i)
            inner = s16(2 * i + 1) * (4.0 if odd is None else 2.0)
            both = now if odd is None else [a + b for a, b in zip(now, last)]
            inside = [inner * both[1], inner * both[2], (inner * (2.0 / 3.0)) * both[3]]
        above = to_upper


def apply_coarse(c, s16, sp8, least, most):
    for i, h in restricted(lambda i: spread(c(i)), None, s16, least, most):
        yield i, pair_sum(h + (sp8(2 * i) + sp8(2 * i + 1)) * c(i))


def coarse_residual(source, u, s16, sp8, least, most):
    for i, h in restricted(lambda i: spread(u(2 * i)), lambda i: spread(u(2 * i + 1)), s16, least, most):
        a, b = 2 * i, 2 * i + 1
        yield i, pair_sum((source(a) - sp8(a) * u(a)) + (source(b) - sp8(b) * u(b)) - h)


class Planes:
    def __init__(self, ref, first, offset=None):
        self.ref, self.first, self.offset = ref, first, offset

    def at(self, p):
        return p - self.first if self.offset is None else p - self.first + self.offset

    def __call__(self, p):
        return self.ref[self.at(p)]

    def put(self, p, v):
        self.ref[self.at(p)] = v


def precondition(source, s16, sp8, dv, steps, work, least, most, emit):
    z, res, c, c1 = work
    lo, hi = (least - 1) // 2, (most + 1) // 2
    for p in range(2 * lo - 5, 2 * hi + 7):
        z.put(p, dv(p) * source(p))
    for i, r in coarse_residual(source, z, s16, sp8, lo - 2, hi + 2):
        res.put(i, r)
        c.put(i, steps(i) * r)
    for old, new, first, last in ((c, c1, lo - 1, hi + 1), (c1, c, lo, hi)):
        for i, a in apply_coarse(old, s16, sp8, first, last):
            new.put(i, old(i) + steps(i) * (res(i) - a))
    for p in range(least - 1, most + 2):
        z.put(p, z(p) + c(p // 2))
    for p, a in apply_fine(z, s16, sp8, least, most):
        emit(p, z(p) + dv(p) * (source(p) - a))


def work_shapes():
    plane = lambda n: pltpu.VMEM((n, *TILE), jnp.float32)
    return [plane(24), plane(12), plane(12), plane(12)]


def work_of(z, res, c, c1):
    return Planes(z, -8), Planes(res, -4), Planes(c, -4), Planes(c1, -4)


def pack_kernel(rhs, classes, supports, out, r, k, s, sems):
    copies = [pltpu.make_async_copy(a, b, sems.at[i]) for i, (a, b) in enumerate(((classes, k), (supports, s), (rhs, r)))]
    for copy in copies:
        copy.start()
    copies[0].wait()
    density = (k[...].astype(jnp.float32) + 1.0) / 4.0
    stiff = 0.001 + density * density * density
    for j in range(0, 16, 2):
        out[j, 0] = stiff
    copies[1].wait()
    support = s[...].astype(jnp.float32)
    for j in range(1, 16, 2):
        out[j, 0] = support
    copies[2].wait()
    for x in range(4):
        for c in range(2):
            v = r[x * 2 + c]
            for h in range(2):
                out[(x * 2 + h) * 2 + c, 1] = v


def my_place():
    pair = lax.axis_index("z") * lax.axis_size("p") + lax.axis_index("p")
    return lax.axis_index("h"), pair, lax.axis_size("z") * lax.axis_size("p")


def grids_kernel(*refs):
    *blocks, out = refs
    for i, ref in enumerate(blocks):
        for j in range(16):
            out[i, j] = ref[j, 0]


def first_kernel(
    own, swap, far, grids, first, applied, s16_out, sp8_out, dv_out, steps_out, out, source_ref, *work
):
    h, pair, pairs = my_place()
    upper_chip = h != 0
    present = (pair > 0, pair >= 0, pair < pairs - 1)

    def plane(refs, p):
        q = p % 8
        h, c = q // 4, (q // 2) % 2
        block = lambda ref: jnp.stack([ref[(x * 2 + h) * 2 + c, q % 2] for x in range(4)])
        if 0 <= p < 8:
            return block(refs[0])
        a, b = block(refs[1]), block(refs[2])
        return jnp.where(upper_chip, b, a) if p < 0 else jnp.where(upper_chip, a, b)

    fields = [ref.at[:, 1] for ref in (own, swap, far)]
    stiffs, supports = ([grids.at[core, i] for i in range(3)] for core in range(2))
    source, s16, sp8, dv = (Planes(r, -8) for r in (source_ref, s16_out, sp8_out, dv_out))
    steps, new = Planes(steps_out, -4), Planes(out, -1)
    for p in range(-7, 15):
        source.put(p, plane(fields, p))
    sums = kept = None
    for p in range(-7, 16):
        t = plane(stiffs, p)
        sp8.put(p, SPRING * plane(supports, p))
        s16.put(p, t * (1.0 / 16.0))
        t = t + after_z(t)
        t = t + after_y(t)
        if sums is not None:
            n = p - 1
            d = sp8(n) + (sums + t) * (1.0 / 3.0)
            ok = present[(n + 8) // 8]
            dv.put(n, jnp.where(ok, OMEGA / d, 0.0))
            if n % 2 and n > -7:
                steps.put(n // 2, jnp.where(ok, DAMP / pair_sum(kept + d), 0.0))
            kept = d
        sums = t

    def emit(p, v):
        new.put(p, v)
        if 0 <= p < 8:
            first[p] = v

    precondition(source, s16, sp8, dv, steps, work_of(*work), -1, 8, emit)
    for p, v in apply_fine(new, s16, sp8, 0, 7):
        applied[p] = v


def second_kernel(first, applied, below, above, s16_ref, sp8_ref, dv_ref, steps_ref, packed, source_ref, *work):
    h, _, _ = my_place()
    shift = h * 4
    for q in range(8):
        source_ref[q] = below[q]
        source_ref[8 + q] = applied[q]
        source_ref[16 + q] = above[q]
    source, s16, sp8, dv = (Planes(r, -8, shift) for r in (source_ref, s16_ref, sp8_ref, dv_ref))
    steps = Planes(steps_ref, -4, h * 2)

    def put(field, p, v):
        for x in range(4):
            packed[x * 2 + p // 2, field, p % 2] = v[x]

    for p in range(4):
        put(0, p, first[shift + p])
        put(1, p, applied[shift + p])
    precondition(source, s16, sp8, dv, steps, work_of(*work), 0, 3, lambda p, v: put(2, p, v))


def rows_of(ref, field, fields):
    return jnp.concatenate(
        [ref[pl.ds(field * 16 + t, FIELDS, stride=fields * 16), :] for t in range(16)], axis=1
    )


def gram_kernel(parts, rhs, out):
    f, a, n = (rows_of(parts, k, 3) for k in range(3))
    r = rows_of(rhs, 0, 1)
    left = jnp.concatenate([f, a], axis=0)
    right = jnp.concatenate([a, r, n, f, jnp.zeros((LANES - 32, 2048), jnp.float32)], axis=0)
    g = lax.dot_general(left, right, (((1,), (1,)), ((), ())), precision=HIGHEST, preferred_element_type=jnp.float32)
    lane = iota(1, (8, LANES))
    tile = jnp.where(lane < 16, g[:8], jnp.where(lane < 32, g[8:], 0.0))
    turned = [tile] + [pltpu.roll(tile, 32 * m, 1) for m in range(1, 4)]
    short = jnp.concatenate([sum(turned[m][k + m : k + m + 1] for m in range(4)) for k in (0, 4)], axis=0)
    for k in range(out.shape[0]):
        out[k] = short


def final_kernel(sums, parts, rhs, sol, resid, direction):
    w = sums[0]
    for k in range(1, sums.shape[0]):
        w = w + sums[k]
    turned = [w] + [pltpu.roll(w, LANES - 32 * m, 1) for m in range(1, 4)]
    w = jnp.concatenate([turned[m][k : k + 1] for k in range(2) for m in range(4)], axis=0)
    shape = (8, LANES)
    lane, row = iota(1, shape), iota(0, shape)
    w = jnp.where(lane < 8, 0.5 * (w + pltpu.roll(w, LANES - 24, 1)), w)
    columns = [jnp.broadcast_to(w[:, k : k + 1], shape) for k in range(8)]
    scale = jnp.ones(shape, jnp.float32)
    for k in range(8):
        inverse = 1.0 / columns[k][k : k + 1, :]
        scale = jnp.where(row == k, inverse, scale)
        factor = jnp.where(row == k, 0.0, columns[k] * inverse)
        for j in range(k + 1, 8):
            columns[j] = columns[j] - factor * columns[j][k : k + 1, :]
        w = w - factor * w[k : k + 1, :]
    w = w * scale
    coef = jnp.where((lane >= 8) & (lane < 16), w, 0.0)
    turn = -pltpu.roll(w, LANES - 16, 1)
    for k in range(8):
        turn = turn + w[:, 16 + k : 17 + k] * coef[k : k + 1, :]
    turn = jnp.where((lane >= 8) & (lane < 16), turn, 0.0)
    weights = jnp.concatenate(
        [pltpu.roll(coef, LANES - 8, 1) + pltpu.roll(turn, 8, 1), -coef, -pltpu.roll(coef, 8, 1)], axis=0
    )[:, :24]
    f, a, n = (rows_of(parts, k, 3) for k in range(3))
    fields = jnp.concatenate([f, a, n], axis=0)
    new = lax.dot_general(weights, fields, (((0,), (0,)), ((), ())), precision=HIGHEST, preferred_element_type=jnp.float32)
    r = rows_of(rhs, 0, 1)
    for ref, v in ((sol, new[:8]), (resid, r + new[8:16]), (direction, f + new[16:24])):
        for t in range(16):
            ref[pl.ds(t, FIELDS, stride=16), :] = v[:, LANES * t : LANES * t + LANES]


def f32(*shape):
    return jax.ShapeDtypeStruct(shape, jnp.float32)


def local(rhs, classes, supports):
    sizes = {a: lax.axis_size(a) for a in ("z", "p", "h", "c", "x")}
    chips = sizes["z"] * sizes["p"] * 2
    chip = ("z", "p", "h")

    packed = pl.pallas_call(
        pack_kernel,
        out_shape=f32(16, 2, 2, 8, LANES),
        in_specs=[pl.BlockSpec(memory_space=pltpu.HBM)] * 3,
        out_specs=vmem(1)[0],
        scratch_shapes=[
            pltpu.VMEM((8, 2, 8, LANES), jnp.float32),
            pltpu.VMEM((2, 8, LANES), jnp.int32),
            pltpu.VMEM((2, 8, LANES), jnp.int32),
            pltpu.SemaphoreType.DMA((3,)),
        ],
        compiler_params=WIDE,
    )(rhs, classes, supports)
    own = lax.all_to_all(packed, ("x", "h", "c"), 0, 0)

    def moved(v, sources):
        return lax.ppermute(v, chip, [(s, i) for i, s in enumerate(sources) if 0 <= s < chips])

    far = moved(own, [i + 2 if i % 2 == 0 else i - 2 for i in range(chips)])
    swap = moved(own, [i - 1 if i % 2 == 0 else i + 1 for i in range(chips)])

    def both_cores(*blocks):
        n = len(blocks)
        grids = pl.pallas_call(
            grids_kernel,
            out_shape=f32(n, 16, 2, 8, LANES),
            in_specs=vmem(n),
            out_specs=vmem(1)[0],
            compiler_params=PARAMS,
        )(*blocks)
        return lax.all_gather(grids, "c")

    grids = both_cores(own, swap, far)
    first, applied, *coefs = pl.pallas_call(
        first_kernel,
        out_shape=[f32(8, *TILE)] * 2 + [f32(24, *TILE)] * 3 + [f32(12, *TILE)],
        in_specs=vmem(4),
        out_specs=vmem(6),
        scratch_shapes=[pltpu.VMEM((10, *TILE), jnp.float32), pltpu.VMEM((24, *TILE), jnp.float32)] + work_shapes(),
        compiler_params=PARAMS,
    )(own, swap, far, grids)
    below = moved(applied, [i - 2 for i in range(chips)])
    above = moved(applied, [i + 2 for i in range(chips)])
    results = pl.pallas_call(
        second_kernel,
        out_shape=f32(8, 3, 2, 8, LANES),
        in_specs=vmem(8),
        out_specs=vmem(1)[0],
        scratch_shapes=[pltpu.VMEM((24, *TILE), jnp.float32)] + work_shapes(),
        compiler_params=PARAMS,
    )(first, applied, below, above, *coefs)
    parts = lax.all_to_all(results, ("x", "c"), 0, 0).reshape(8 * 48, LANES)
    rows = rhs.reshape(8 * 16, LANES)

    tile = pl.pallas_call(
        gram_kernel, out_shape=f32(sizes["p"] * 4 * sizes["x"], 2, LANES), in_specs=vmem(2), out_specs=vmem(1)[0], compiler_params=PARAMS
    )(parts, rows)
    tile = lax.all_to_all(tile, ("p", "h", "c", "x"), 0, 0).sum(0)
    tile = jnp.broadcast_to(tile, (sizes["z"], 2, LANES))
    tile = lax.all_to_all(tile, "z", 0, 0)
    outs = pl.pallas_call(
        final_kernel,
        out_shape=[f32(128, LANES)] * 3,
        in_specs=vmem(3),
        out_specs=vmem(3),
        compiler_params=PARAMS,
    )(tile, parts, rows)
    return tuple(v.reshape(8, 2, 8, LANES) for v in outs)


def solution(mesh):
    gx, gy = mesh.shape["gx"], mesh.shape["gy"]
    y = min(8, gx // 2)
    fine = Mesh(mesh.devices.reshape(gx // (2 * y), y // 2, 2, 2, gy), ("z", "p", "h", "c", "x"))
    across = ("z", "p", "h", "c")
    grid = P(across, "x", None)
    fields = P(None, across, "x", None)
    return jax.shard_map(
        local, mesh=fine, in_specs=(fields, grid, grid), out_specs=(fields,) * 3, check_vma=False
    )
```

```python
import jax
import jax.numpy as jnp
from jax import lax
from jax.experimental import pallas as pl
from jax.experimental.pallas import tpu as pltpu
from jax.sharding import Mesh, PartitionSpec as P

SPRING = 8.0
OMEGA = 0.6
DAMP = 0.5
LANES = 128
FIELDS = 8
TILE = (4, 8, LANES)
HIGHEST = lax.Precision.HIGHEST
PARAMS = pltpu.CompilerParams(vmem_limit_bytes=24 * 1024 * 1024)
WIDE = pltpu.CompilerParams(vmem_limit_bytes=62 * 1024 * 1024)


def vmem(n):
    return [pl.BlockSpec(memory_space=pltpu.VMEM)] * n


def iota(axis, shape=TILE):
    return lax.broadcasted_iota(jnp.int32, shape, axis)


def before_z(v):
    return jnp.where(iota(2) == 0, 0.0, pltpu.roll(v, 1, 2))


def after_z(v):
    return jnp.where(iota(2) == LANES - 1, 0.0, pltpu.roll(v, LANES - 1, 2))


def before_y(v):
    r = pltpu.roll(v, 1, 1)
    return jnp.where(iota(1) == 0, jnp.concatenate([jnp.zeros_like(r[:1]), r[:3]], axis=0), r)


def after_y(v):
    r = pltpu.roll(v, 7, 1)
    return jnp.where(iota(1) == 7, jnp.concatenate([r[1:], jnp.zeros_like(r[:1])], axis=0), r)


def pair_sum(v):
    v = (v + jnp.where(iota(1) % 2 == 0, pltpu.roll(v, 7, 1), pltpu.roll(v, 1, 1))).reshape(32, LANES)
    square = (LANES, LANES)
    ones = (iota(0, square) // 2 == iota(1, square) // 2).astype(jnp.bfloat16)
    high = v.astype(jnp.bfloat16)
    rest = v - high.astype(jnp.float32)
    middle = rest.astype(jnp.bfloat16)
    low = (rest - middle.astype(jnp.float32)).astype(jnp.bfloat16)
    pieces = jnp.concatenate([high, middle, low], axis=1)
    ones = jnp.concatenate([ones] * 3, axis=0)
    return jnp.dot(pieces, ones, preferred_element_type=jnp.float32).reshape(TILE)


def spread(u):
    low = before_z(u)
    out = []
    for f in (u + low, u - low):
        g = before_y(f)
        out += [f + g, f - g]
    return out


def element_plane(lower, upper, s16):
    s24, s48 = s16 * (2.0 / 3.0), s16 * (1.0 / 3.0)
    ss, ds, sd, dd = [(b + a, b - a) for a, b in zip(lower, upper)]
    w = ((s16 * ds[0], s24 * ds[1]), (s16 * sd[0], s24 * sd[1]), (s24 * dd[0], s48 * dd[1]))
    v = s16 * ss[1]
    return [-v] + [a - b for a, b in w], [v] + [a + b for a, b in w]


def gather(n):
    ss, ds, sd, dd = n
    ms = (ss + ds) + after_y(ss - ds)
    md = (sd + dd) + after_y(sd - dd)
    return (ms + md) + after_z(ms - md)


def apply_fine(u, s16, sp8, least, most):
    last, above = spread(u(least - 1)), None
    for e in range(least, most + 2):
        now = spread(u(e))
        to_lower, to_upper = element_plane(last, now, s16(e))
        if above is not None:
            yield e - 1, gather([a + b for a, b in zip(above, to_lower)]) + sp8(e - 1) * u(e - 1)
        last, above = now, to_upper


def restricted(even, odd, s16, least, most):
    last, above = (even if odd is None else odd)(least - 1), None
    for i in range(least, most + 2):
        now = even(i)
        to_lower, to_upper = element_plane(last, now, s16(2 * i))
        if above is not None:
            n = [a + b for a, b in zip(above, to_lower)]
            yield i - 1, gather([n[0]] + [a + b for a, b in zip(n[1:], inside)])
        if i <= most:
            last = now if odd is None else odd(i)
            inner = s16(2 * i + 1) * (4.0 if odd is None else 2.0)
            both = now if odd is None else [a + b for a, b in zip(now, last)]
            inside = [inner * both[1], inner * both[2], (inner * (2.0 / 3.0)) * both[3]]
        above = to_upper


def apply_coarse(c, s16, sp8, least, most):
    for i, h in restricted(lambda i: spread(c(i)), None, s16, least, most):
        yield i, pair_sum(h + (sp8(2 * i) + sp8(2 * i + 1)) * c(i))


def coarse_residual(source, u, s16, sp8, least, most):
    for i, h in restricted(lambda i: spread(u(2 * i)), lambda i: spread(u(2 * i + 1)), s16, least, most):
        a, b = 2 * i, 2 * i + 1
        yield i, pair_sum((source(a) - sp8(a) * u(a)) + (source(b) - sp8(b) * u(b)) - h)


class Planes:
    def __init__(self, ref, first, offset=None):
        self.ref, self.first, self.offset = ref, first, offset

    def at(self, p):
        return p - self.first if self.offset is None else p - self.first + self.offset

    def __call__(self, p):
        return self.ref[self.at(p)]

    def put(self, p, v):
        self.ref[self.at(p)] = v


def precondition(source, s16, sp8, dv, steps, work, least, most, emit):
    z, res, c, c1 = work
    lo, hi = (least - 1) // 2, (most + 1) // 2
    for p in range(2 * lo - 5, 2 * hi + 7):
        z.put(p, dv(p) * source(p))
    for i, r in coarse_residual(source, z, s16, sp8, lo - 2, hi + 2):
        res.put(i, r)
        c.put(i, steps(i) * r)
    for old, new, first, last in ((c, c1, lo - 1, hi + 1), (c1, c, lo, hi)):
        for i, a in apply_coarse(old, s16, sp8, first, last):
            new.put(i, old(i) + steps(i) * (res(i) - a))
    for p in range(least - 1, most + 2):
        z.put(p, z(p) + c(p // 2))
    for p, a in apply_fine(z, s16, sp8, least, most):
        emit(p, z(p) + dv(p) * (source(p) - a))


def work_shapes():
    plane = lambda n: pltpu.VMEM((n, *TILE), jnp.float32)
    return [plane(24), plane(12), plane(12), plane(12)]


def work_of(z, res, c, c1):
    return Planes(z, -8), Planes(res, -4), Planes(c, -4), Planes(c1, -4)


def pack_kernel(rhs, classes, supports, out, r, k, s, sems):
    copies = [pltpu.make_async_copy(a, b, sems.at[i]) for i, (a, b) in enumerate(((classes, k), (supports, s), (rhs, r)))]
    for copy in copies:
        copy.start()
    copies[0].wait()
    density = (k[...].astype(jnp.float32) + 1.0) / 4.0
    stiff = 0.001 + density * density * density
    for j in range(0, 16, 2):
        out[j, 0] = stiff
    copies[1].wait()
    support = s[...].astype(jnp.float32)
    for j in range(1, 16, 2):
        out[j, 0] = support
    copies[2].wait()
    for x in range(4):
        for c in range(2):
            v = r[x * 2 + c]
            for h in range(2):
                out[(x * 2 + h) * 2 + c, 1] = v


def my_place():
    pair = lax.axis_index("z") * lax.axis_size("p") + lax.axis_index("p")
    return lax.axis_index("h"), pair, lax.axis_size("z") * lax.axis_size("p")


def grids_kernel(*refs):
    *blocks, out = refs
    for i, ref in enumerate(blocks):
        for j in range(16):
            out[i, j] = ref[j, 0]


def first_kernel(
    own, swap, far, grids, first, applied, s16_out, sp8_out, dv_out, steps_out, out, source_ref, *work
):
    h, pair, pairs = my_place()
    upper_chip = h != 0
    present = (pair > 0, pair >= 0, pair < pairs - 1)

    def plane(refs, p):
        q = p % 8
        h, c = q // 4, (q // 2) % 2
        block = lambda ref: jnp.stack([ref[(x * 2 + h) * 2 + c, q % 2] for x in range(4)])
        if 0 <= p < 8:
            return block(refs[0])
        a, b = block(refs[1]), block(refs[2])
        return jnp.where(upper_chip, b, a) if p < 0 else jnp.where(upper_chip, a, b)

    fields = [ref.at[:, 1] for ref in (own, swap, far)]
    stiffs, supports = ([grids.at[core, i] for i in range(3)] for core in range(2))
    source, s16, sp8, dv = (Planes(r, -8) for r in (source_ref, s16_out, sp8_out, dv_out))
    steps, new = Planes(steps_out, -4), Planes(out, -1)
    for p in range(-7, 15):
        source.put(p, plane(fields, p))
    sums = kept = None
    for p in range(-7, 16):
        t = plane(stiffs, p)
        sp8.put(p, SPRING * plane(supports, p))
        s16.put(p, t * (1.0 / 16.0))
        t = t + after_z(t)
        t = t + after_y(t)
        if sums is not None:
            n = p - 1
            d = sp8(n) + (sums + t) * (1.0 / 3.0)
            ok = present[(n + 8) // 8]
            dv.put(n, jnp.where(ok, OMEGA / d, 0.0))
            if n % 2 and n > -7:
                steps.put(n // 2, jnp.where(ok, DAMP / pair_sum(kept + d), 0.0))
            kept = d
        sums = t

    def emit(p, v):
        new.put(p, v)
        if 0 <= p < 8:
            first[p] = v

    precondition(source, s16, sp8, dv, steps, work_of(*work), -1, 8, emit)
    for p, v in apply_fine(new, s16, sp8, 0, 7):
        applied[p] = v


def second_kernel(first, applied, below, above, s16_ref, sp8_ref, dv_ref, steps_ref, packed, source_ref, *work):
    h, _, _ = my_place()
    shift = h * 4
    for q in range(8):
        source_ref[q] = below[q]
        source_ref[8 + q] = applied[q]
        source_ref[16 + q] = above[q]
    source, s16, sp8, dv = (Planes(r, -8, shift) for r in (source_ref, s16_ref, sp8_ref, dv_ref))
    steps = Planes(steps_ref, -4, h * 2)

    def put(field, p, v):
        for x in range(4):
            packed[x * 2 + p // 2, field, p % 2] = v[x]

    for p in range(4):
        put(0, p, first[shift + p])
        put(1, p, applied[shift + p])
    precondition(source, s16, sp8, dv, steps, work_of(*work), 0, 3, lambda p, v: put(2, p, v))


def rows_of(ref, field, fields):
    return jnp.concatenate(
        [ref[pl.ds(field * 16 + t, FIELDS, stride=fields * 16), :] for t in range(16)], axis=1
    )


def gram_kernel(parts, rhs, out):
    f, a, n = (rows_of(parts, k, 3) for k in range(3))
    r = rows_of(rhs, 0, 1)
    left = jnp.concatenate([f, a], axis=0)
    right = jnp.concatenate([a, r, n, f, jnp.zeros((LANES - 32, 2048), jnp.float32)], axis=0)
    g = lax.dot_general(left, right, (((1,), (1,)), ((), ())), precision=HIGHEST, preferred_element_type=jnp.float32)
    lane = iota(1, (8, LANES))
    tile = jnp.where(lane < 16, g[:8], jnp.where(lane < 32, g[8:], 0.0))
    turned = [tile] + [pltpu.roll(tile, 32 * m, 1) for m in range(1, 4)]
    short = jnp.concatenate([sum(turned[m][k + m : k + m + 1] for m in range(4)) for k in (0, 4)], axis=0)
    for k in range(out.shape[0]):
        out[k] = short


def final_kernel(sums, parts, rhs, sol, resid, direction):
    w = sums[0]
    for k in range(1, sums.shape[0]):
        w = w + sums[k]
    turned = [w] + [pltpu.roll(w, LANES - 32 * m, 1) for m in range(1, 4)]
    w = jnp.concatenate([turned[m][k : k + 1] for k in range(2) for m in range(4)], axis=0)
    shape = (8, LANES)
    lane, row = iota(1, shape), iota(0, shape)
    w = jnp.where(lane < 8, 0.5 * (w + pltpu.roll(w, LANES - 24, 1)), w)
    columns = [jnp.broadcast_to(w[:, k : k + 1], shape) for k in range(8)]
    scale = jnp.ones(shape, jnp.float32)
    for k in range(8):
        inverse = 1.0 / columns[k][k : k + 1, :]
        scale = jnp.where(row == k, inverse, scale)
        factor = jnp.where(row == k, 0.0, columns[k] * inverse)
        for j in range(k + 1, 8):
            columns[j] = columns[j] - factor * columns[j][k : k + 1, :]
        w = w - factor * w[k : k + 1, :]
    w = w * scale
    coef = jnp.where((lane >= 8) & (lane < 16), w, 0.0)
    turn = -pltpu.roll(w, LANES - 16, 1)
    for k in range(8):
        turn = turn + w[:, 16 + k : 17 + k] * coef[k : k + 1, :]
    turn = jnp.where((lane >= 8) & (lane < 16), turn, 0.0)
    weights = jnp.concatenate(
        [pltpu.roll(coef, LANES - 8, 1) + pltpu.roll(turn, 8, 1), -coef, -pltpu.roll(coef, 8, 1)], axis=0
    )[:, :24]
    f, a, n = (rows_of(parts, k, 3) for k in range(3))
    fields = jnp.concatenate([f, a, n], axis=0)
    new = lax.dot_general(weights, fields, (((0,), (0,)), ((), ())), precision=HIGHEST, preferred_element_type=jnp.float32)
    r = rows_of(rhs, 0, 1)
    for ref, v in ((sol, new[:8]), (resid, r + new[8:16]), (direction, f + new[16:24])):
        for t in range(16):
            ref[pl.ds(t, FIELDS, stride=16), :] = v[:, LANES * t : LANES * t + LANES]


def f32(*shape):
    return jax.ShapeDtypeStruct(shape, jnp.float32)


def local(rhs, classes, supports):
    sizes = {a: lax.axis_size(a) for a in ("z", "p", "h", "c", "x")}
    chips = sizes["z"] * sizes["p"] * 2
    chip = ("z", "p", "h")

    packed = pl.pallas_call(
        pack_kernel,
        out_shape=f32(16, 2, 2, 8, LANES),
        in_specs=[pl.BlockSpec(memory_space=pltpu.HBM)] * 3,
        out_specs=vmem(1)[0],
        scratch_shapes=[
            pltpu.VMEM((8, 2, 8, LANES), jnp.float32),
            pltpu.VMEM((2, 8, LANES), jnp.int32),
            pltpu.VMEM((2, 8, LANES), jnp.int32),
            pltpu.SemaphoreType.DMA((3,)),
        ],
        compiler_params=WIDE,
    )(rhs, classes, supports)
    own = lax.all_to_all(packed, ("x", "h", "c"), 0, 0)

    def moved(v, sources):
        return lax.ppermute(v, chip, [(s, i) for i, s in enumerate(sources) if 0 <= s < chips])

    far = moved(own, [i + 2 if i % 2 == 0 else i - 2 for i in range(chips)])
    swap = moved(own, [i - 1 if i % 2 == 0 else i + 1 for i in range(chips)])

    def both_cores(*blocks):
        n = len(blocks)
        grids = pl.pallas_call(
            grids_kernel,
            out_shape=f32(n, 16, 2, 8, LANES),
            in_specs=vmem(n),
            out_specs=vmem(1)[0],
            compiler_params=PARAMS,
        )(*blocks)
        return lax.all_gather(grids, "c")

    grids = both_cores(own, swap, far)
    first, applied, *coefs = pl.pallas_call(
        first_kernel,
        out_shape=[f32(8, *TILE)] * 2 + [f32(24, *TILE)] * 3 + [f32(12, *TILE)],
        in_specs=vmem(4),
        out_specs=vmem(6),
        scratch_shapes=[pltpu.VMEM((10, *TILE), jnp.float32), pltpu.VMEM((24, *TILE), jnp.float32)] + work_shapes(),
        compiler_params=PARAMS,
    )(own, swap, far, grids)
    below = moved(applied, [i - 2 for i in range(chips)])
    above = moved(applied, [i + 2 for i in range(chips)])
    results = pl.pallas_call(
        second_kernel,
        out_shape=f32(8, 3, 2, 8, LANES),
        in_specs=vmem(8),
        out_specs=vmem(1)[0],
        scratch_shapes=[pltpu.VMEM((24, *TILE), jnp.float32)] + work_shapes(),
        compiler_params=PARAMS,
    )(first, applied, below, above, *coefs)
    parts = lax.all_to_all(results, ("x", "c"), 0, 0).reshape(8 * 48, LANES)
    rows = rhs.reshape(8 * 16, LANES)

    tile = pl.pallas_call(
        gram_kernel, out_shape=f32(sizes["z"], 2, LANES), in_specs=vmem(2), out_specs=vmem(1)[0], compiler_params=PARAMS
    )(parts, rows)
    tile = lax.all_to_all(tile, "z", 0, 0).sum(0)
    tile = jnp.broadcast_to(tile, (sizes["p"] * 4 * sizes["x"], 2, LANES))
    tile = lax.all_to_all(tile, ("p", "h", "c", "x"), 0, 0)
    outs = pl.pallas_call(
        final_kernel,
        out_shape=[f32(128, LANES)] * 3,
        in_specs=vmem(3),
        out_specs=vmem(3),
        compiler_params=PARAMS,
    )(tile, parts, rows)
    return tuple(v.reshape(8, 2, 8, LANES) for v in outs)


def solution(mesh):
    gx, gy = mesh.shape["gx"], mesh.shape["gy"]
    y = min(8, gx // 2)
    fine = Mesh(mesh.devices.reshape(gx // (2 * y), y // 2, 2, 2, gy), ("z", "p", "h", "c", "x"))
    across = ("z", "p", "h", "c")
    grid = P(across, "x", None)
    fields = P(None, across, "x", None)
    return jax.shard_map(
        local, mesh=fine, in_specs=(fields, grid, grid), out_specs=(fields,) * 3, check_vma=False
    )
```
